1024 devices in a mesh: node: 64 (over z_hi, x, core), local: 16 (over z_lo, y).
Axes of the slice: x: 8, y: 8, z: 8 (z_hi: 4, z_lo: 2; z = z_hi * 2 + z_lo), core: 2. Of those that a mesh axis runs over, the one named last changes fastest.
Arguments:
- tokens: bfloat16 [2048, 6144], P(None, 'local'), may hold values from -6 to 6
- codes: bfloat16 [6144, 24576], P('local', 'node'), may hold values from -4 to 4
- scales: float32 [3, 24576], P(None, 'node'), may hold values from 0.008 to 0.02
- cotangent: bfloat16 [2048, 24576], P('local', 'node'), may hold values from -16 to 16
Outputs:
- activated: bfloat16 [2048, 24576], P('local', 'node')
- input_grad: bfloat16 [2048, 6144], P('node', 'local')
- weight_grad: float32 [6144, 24576], P('local', 'node')
The draws below stay inside these ranges and needn't reach their ends.
All inputs are finite; a program needn't handle non-finite values.
Results may differ from the reference program's by a relative error of at most 0.0063.
Values may be sent and summed in bfloat16 or wider, within the bound.
No kernel may reach another device: no remote copies, remote signals or barrier semaphores. Data moves between devices by JAX's collectives and lax.ppermute only.
A program may use at most 64 MiB of HBM per device.

```python
import math
import jax
import jax.numpy as jnp
from jax import lax

D = 6144
BLOCK = 2048
TOKENS = 2048
FF = 24576
NBLK = 3


def strengthened(result, rng, source, target, parts, factor):
    owner, partner = [(jnp.arange(result.shape[axis_at]) // (result.shape[axis_at] // parts)).reshape([-1 if axis == axis_at else 1 for axis in range(result.ndim)]) for axis_at in (source, target)]
    chosen = jax.random.permutation(rng, parts)[partner]
    strong = (owner == chosen) | (owner == (partner + parts // 2) % parts)
    return jnp.where(strong, factor * result, result)


def block_scale(own_key, extent, cuts, least, largest):
    level, own = 1.0, jax.random.fold_in(own_key, 6)
    for position, parts in cuts:
        draws = jnp.exp(jax.random.uniform(jax.random.fold_in(own, position), (parts,), jnp.float32, least / len(cuts), largest / len(cuts)))
        level = level * jnp.repeat(draws, extent[position] // parts).reshape([-1 if axis == position else 1 for axis in range(len(extent))])
    return level


def centred(rng, extent, width, most, pieces=(), dtype=jnp.bfloat16):
    result = jax.random.normal(rng, extent, jnp.float32) * width
    if len(pieces) > 0:
        result = block_scale(rng, extent, pieces, -0.22, 0.18) * result
    return jnp.clip(result, min=-most, max=most).astype(dtype)


def gaussian_with(own_key, extent, width, reach, split, heavy, kind=jnp.bfloat16):
    array = width * jax.random.normal(own_key, extent, jnp.float32)
    if split:
        array = array * block_scale(own_key, extent, split, -0.22, 0.18)
    return jnp.clip(strengthened(array, jax.random.fold_in(own_key, 3), *heavy), -reach, reach).astype(kind)


def setup_inputs(seed: int = 0) -> dict:
    seeds = jax.random.split(jax.random.key(seed), 5)
    return {
        "tokens": gaussian_with(seeds[0], (TOKENS, D), 1.0, 6.0, ((1, 16),), (1, 0, 16, 2.0)),
        "codes": centred(seeds[1], (D, FF), 1.0, 4.0, ((0, 16), (1, 64))),
        "scales": jnp.clip(jnp.exp(math.log(0.02) - 0.91629066 * jax.random.uniform(seeds[2], (NBLK, FF), jnp.float32) ** block_scale(seeds[2], (NBLK, FF), ((1, 64),), -0.2, 0.2)), 0.008, 0.02),
        "cotangent": gaussian_with(seeds[3], (TOKENS, FF), 1.0, 16.0, ((0, 16), (1, 64)), (1, 0, 64, 4.0)),
    }


def gelu_tanh(value):
    inner = math.sqrt(2.0 / math.pi) * (value + 0.044715 * value * value * value)
    return 0.5 * value * (1.0 + jnp.tanh(inner))

def reference(tokens, codes, scales, cotangent):
    row_block = (jnp.arange(D) // BLOCK).astype(jnp.int32)
    weight = (codes.astype(jnp.float32) * scales[row_block, :]).astype(jnp.bfloat16)
    pre = jnp.dot(tokens, weight, preferred_element_type=jnp.float32)
    act, pull = jax.vjp(gelu_tanh, pre)
    slope = pull(cotangent.astype(jnp.float32))[0].astype(jnp.bfloat16)
    input_grad = lax.dot_general(slope, weight, (((1,), (1,)), ((), ())), preferred_element_type=jnp.float32)
    weight_grad = lax.dot_general(tokens, slope, (((0,), (0,)), ((), ())), preferred_element_type=jnp.float32)
    weight_grad = weight_grad * TOKENS ** (-0.5)
    return (act.astype(jnp.bfloat16), input_grad.astype(jnp.bfloat16), weight_grad)
```

```python
import math

import jax
import jax.numpy as jnp
from jax import lax
from jax.sharding import PartitionSpec as P

BLOCK = 2048
F32 = jnp.float32
BF16 = jnp.bfloat16


def gelu_tanh(value):
    inner = math.sqrt(2.0 / math.pi) * (value + 0.044715 * value * value * value)
    return 0.5 * value * (1.0 + jnp.tanh(inner))


def dequant(piece, start, scales):
    block = (start + lax.broadcasted_iota(jnp.int32, piece.shape, 0)) // BLOCK
    scale = jnp.broadcast_to(scales[0:1], piece.shape)
    for i in range(1, scales.shape[0]):
        scale = jnp.where(block == i, scales[i : i + 1], scale)
    return (piece.astype(F32) * scale).astype(BF16)


def shards(locals_, nodes, tokens, codes, scales, cotangent):
    rows = tokens.shape[0]
    feat = codes.shape[0]
    units = codes.shape[1]
    mine = rows // locals_
    out_rows = rows // nodes
    weight = dequant(codes, lax.axis_index("local") * feat, scales)
    partial = jnp.dot(tokens, weight, preferred_element_type=F32).astype(BF16)
    partial = partial.reshape(locals_, mine, units)
    partial = lax.all_to_all(partial, "local", 0, 0, tiled=True)
    pre = jnp.sum(partial.astype(F32), axis=0)
    act, pull = jax.vjp(gelu_tanh, pre)
    slope = pull(cotangent.astype(F32))[0].astype(BF16)
    spread = jnp.broadcast_to(slope[None], (locals_, mine, units))
    spread = lax.all_to_all(spread, "local", 0, 0, tiled=True)
    slope_full = spread.reshape(rows, units)
    core = lax.axis_index("node") % 2
    by_core = slope_full.reshape(nodes // 2, 2, out_rows, units)

    def grad_rows(which):
        part = lax.dynamic_index_in_dim(by_core, which, 1, keepdims=False)
        return lax.dot_general(
            part.reshape(rows // 2, units),
            weight,
            (((1,), (1,)), ((), ())),
            preferred_element_type=F32,
        )

    other = lax.ppermute(
        grad_rows(1 - core).astype(BF16), "node", [(i, i ^ 1) for i in range(nodes)]
    )
    both = (grad_rows(core) + other.astype(F32)).astype(BF16)
    both = both.reshape(nodes // 2, out_rows, feat)
    groups = [list(range(c, nodes, 2)) for c in range(2)]
    both = lax.all_to_all(both, "node", 0, 0, axis_index_groups=groups, tiled=True)
    input_grad = jnp.sum(both.astype(F32), axis=0).astype(BF16)
    weight_grad = lax.dot_general(
        tokens, slope_full, (((0,), (0,)), ((), ())), preferred_element_type=F32
    ) * (rows ** (-0.5))
    return act.astype(BF16), input_grad, weight_grad


def solution(mesh):
    locals_, nodes = mesh.shape["local"], mesh.shape["node"]

    def body(*args):
        return shards(locals_, nodes, *args)

    placed = (P(None, "local"), P("local", "node"), P(None, "node"), P("local", "node"))
    return jax.shard_map(
        body,
        mesh=mesh,
        in_specs=placed,
        out_specs=(P("local", "node"), P("node", "local"), P("local", "node")),
        check_vma=False,
    )
```

```python
import functools
import math

import jax
import jax.numpy as jnp
from jax import lax
from jax.experimental import pallas as pl
from jax.experimental.pallas import tpu as pltpu
from jax.sharding import PartitionSpec as P

BLOCK = 2048
F32 = jnp.float32
BF16 = jnp.bfloat16
ROOT = math.sqrt(2.0 / math.pi)
VMEM = pl.BlockSpec(memory_space=pltpu.VMEM)
SMEM = pl.BlockSpec(memory_space=pltpu.SMEM)


def call(kernel, outs, specs, flops, size, *args):
    return pl.pallas_call(
        kernel,
        out_shape=[jax.ShapeDtypeStruct(s, d) for s, d in outs],
        in_specs=specs,
        out_specs=[VMEM] * len(outs),
        compiler_params=pltpu.CompilerParams(vmem_limit_bytes=40 * 2**20),
        cost_estimate=pl.CostEstimate(flops=flops, bytes_accessed=size, transcendentals=0),
    )(*args)


def project(start_ref, tok_ref, codes_ref, scales_ref, w_ref, out_ref):
    feat, units = codes_ref.shape
    row = start_ref[0] + lax.broadcasted_iota(jnp.int32, (feat, units), 0)
    scale = jnp.broadcast_to(scales_ref[0:1, :], (feat, units))
    for i in range(1, scales_ref.shape[0]):
        scale = jnp.where(row >= i * BLOCK, scales_ref[i : i + 1, :], scale)
    weight = (codes_ref[...].astype(F32) * scale).astype(BF16)
    w_ref[...] = weight
    for q in range(out_ref.shape[0]):
        res = jnp.dot(tok_ref[:, q].reshape(-1, feat), weight, preferred_element_type=F32)
        out_ref[q] = res.astype(BF16).reshape(out_ref.shape[1:])


def activate(side_ref, got_ref, cot_ref, far_cot_ref, act_ref, far_act_ref, slope_ref):
    side = side_ref[0]
    for k, (cots, acts) in enumerate(((cot_ref, act_ref), (far_cot_ref, far_act_ref))):
        which = side if k == 0 else 1 - side
        pre = jnp.sum(got_ref[which].astype(F32), axis=0)
        cot = (cots[side] if k == 0 else cots[...]).astype(F32)
        square = pre * pre
        tanh = jnp.tanh(ROOT * (pre + 0.044715 * square * pre))
        acts[...] = (0.5 * pre * (1.0 + tanh)).astype(BF16)
        inner = ROOT * (1.0 + 3.0 * 0.044715 * square)
        grad = 0.5 * (1.0 + tanh) + 0.5 * pre * (1.0 - tanh * tanh) * inner
        slope = (cot * grad).astype(BF16)
        slope_ref[:, k] = jnp.broadcast_to(slope[None], (slope_ref.shape[0],) + slope.shape)


def back(core, slope_ref, weights):
    total = None
    for k, weight in enumerate(weights):
        rows = slope_ref[:, k, core]
        part = lax.dot_general(
            rows.reshape(-1, rows.shape[-1]),
            weight[...],
            (((1,), (1,)), ((), ())),
            preferred_element_type=F32,
        )
        total = part if total is None else total + part
    return total


def back_other(core_ref, slope_ref, w_ref, far_w_ref, out_ref):
    out_ref[...] = back(1 - core_ref[0], slope_ref, (w_ref, far_w_ref)).astype(BF16)


def back_mine(core_ref, slope_ref, w_ref, far_w_ref, other_ref, out_ref):
    total = back(core_ref[0], slope_ref, (w_ref, far_w_ref)) + other_ref[...].astype(F32)
    out_ref[...] = total.astype(BF16).reshape(out_ref.shape)


def finish(got_ref, out_ref):
    out_ref[...] = jnp.sum(got_ref[...].astype(F32), axis=0).astype(BF16)


def outer(side, tok_ref, slope_ref, k):
    rows = tok_ref[:, side]
    grads = slope_ref[:, k]
    return lax.dot_general(
        rows.reshape(-1, rows.shape[-1]),
        grads.reshape(-1, grads.shape[-1]),
        (((0,), (0,)), ((), ())),
        preferred_element_type=F32,
    )


def weigh_far(side_ref, tok_ref, slope_ref, out_ref):
    out_ref[...] = outer(side_ref[0], tok_ref, slope_ref, 1).astype(BF16)


def weigh_own(factor, side_ref, tok_ref, slope_ref, far_ref, out_ref):
    total = outer(side_ref[0], tok_ref, slope_ref, 0) + far_ref[...].astype(F32)
    out_ref[...] = total * factor


def shards(locals_, nodes, tokens, codes, scales, cotangent):
    rows, feat = tokens.shape
    units = codes.shape[1]
    per = nodes // locals_
    each = rows // nodes
    half = rows // locals_ // 2
    node = lax.axis_index("node").astype(jnp.int32)
    start = (lax.axis_index("local").astype(jnp.int32) * feat).reshape(1)
    core = (node % 2).reshape(1)
    side = (node // 2 % 2).reshape(1)
    tok = tokens.reshape(locals_, 2, half, feat)
    cot = cotangent.reshape(2, half, units)
    pair = [(i, i ^ 2) for i in range(nodes)]
    flops = 2 * rows * feat * units
    size = 2 * rows * feat

    weight, partial = call(
        project,
        [((feat, units), BF16), ((2, locals_, half, units), BF16)],
        [SMEM, VMEM, VMEM, VMEM],
        flops, 2 * size,
        start, tok, codes, scales,
    )
    members = [
        [(n + 2 * q) * locals_ + l for q in range(2) for l in range(locals_)]
        for n in range(nodes)
        if n & 2 == 0
    ]
    got = lax.all_to_all(
        partial.reshape(2 * locals_, half, units),
        ("node", "local"), 0, 0, axis_index_groups=members, tiled=True,
    ).reshape(2, locals_, half, units)
    far_weight = lax.ppermute(weight, "node", pair)
    far_cot = lax.ppermute(
        lax.dynamic_index_in_dim(cot, 1 - side[0], 0, False), "node", pair
    )
    act_own, act_far, slope = call(
        activate,
        [((half, units), BF16), ((half, units), BF16), ((locals_, 2, half, units), BF16)],
        [SMEM, VMEM, VMEM, VMEM],
        rows * units * 4, 2 * size,
        side, got, cot, far_cot,
    )
    spread = lax.all_to_all(
        slope.reshape(locals_, 2 * half, units), "local", 0, 0, tiled=True
    )
    by_core = spread.reshape(locals_, 2, 2, each, units)
    by_pair = spread.reshape(locals_, 2, half, units)
    (other,) = call(
        back_other,
        [((rows // 4, feat), BF16)],
        [SMEM, VMEM, VMEM, VMEM],
        flops // 2, size,
        core, by_core, weight, far_weight,
    )
    other = lax.ppermute(other, "node", [(i, i ^ 1) for i in range(nodes)])
    (both,) = call(
        back_mine,
        [((locals_, each, feat), BF16)],
        [SMEM, VMEM, VMEM, VMEM, VMEM],
        flops // 2, size,
        core, by_core, weight, far_weight, other,
    )
    groups = [list(range(c, nodes, per)) for c in range(per)]
    sums = lax.all_to_all(both, "node", 0, 0, axis_index_groups=groups, tiled=True)
    (far_part,) = call(
        weigh_far,
        [((feat, units), BF16)],
        [SMEM, VMEM, VMEM],
        flops // 2, size,
        side, tok, by_pair,
    )
    far_part = lax.ppermute(far_part, "node", pair)
    (weight_grad,) = call(
        functools.partial(weigh_own, rows ** (-0.5)),
        [((feat, units), F32)],
        [SMEM, VMEM, VMEM, VMEM],
        flops // 2, size,
        side, tok, by_pair, far_part,
    )
    (input_grad,) = call(
        finish, [((each, feat), BF16)], [VMEM], rows * feat, size // 4, sums
    )
    act_far = lax.ppermute(act_far, "node", pair)
    first = side[0] == 0
    act = jnp.concatenate(
        [jnp.where(first, act_own, act_far), jnp.where(first, act_far, act_own)], axis=0
    )
    return act, input_grad, weight_grad


def solution(mesh):
    body = functools.partial(shards, mesh.shape["local"], mesh.shape["node"])
    placed = (P(None, "local"), P("local", "node"), P(None, "node"), P("local", "node"))
    return jax.shard_map(
        lambda *args: body(*args),
        mesh=mesh,
        in_specs=placed,
        out_specs=(P("local", "node"), P("node", "local"), P("local", "node")),
        check_vma=False,
    )
```

```python
import functools
import math

import jax
import jax.numpy as jnp
from jax import lax
from jax.experimental import pallas as pl
from jax.experimental.pallas import tpu as pltpu
from jax.sharding import PartitionSpec as P

BLOCK = 2048
F32 = jnp.float32
BF16 = jnp.bfloat16
ROOT = math.sqrt(2.0 / math.pi)
VMEM = pl.BlockSpec(memory_space=pltpu.VMEM)
SMEM = pl.BlockSpec(memory_space=pltpu.SMEM)


def call(kernel, outs, specs, flops, size, *args):
    return pl.pallas_call(
        kernel,
        out_shape=[jax.ShapeDtypeStruct(s, d) for s, d in outs],
        in_specs=specs,
        out_specs=[VMEM] * len(outs),
        compiler_params=pltpu.CompilerParams(vmem_limit_bytes=40 * 2**20),
        cost_estimate=pl.CostEstimate(flops=flops, bytes_accessed=size, transcendentals=0),
    )(*args)


HBM = pl.BlockSpec(memory_space=pltpu.HBM)


def project(start_ref, tok_hbm, codes_hbm, scales_hbm, w_ref, out_ref, tok_ref, codes_ref, scales_ref, sems):
    feat, units = codes_ref.shape
    cuts = [(z, y) for z in range(2) for y in (0, 1)]
    span = tok_ref.shape[1] // 2
    first = [
        pltpu.make_async_copy(codes_hbm, codes_ref, sems.at[0]),
        pltpu.make_async_copy(scales_hbm, scales_ref, sems.at[1]),
    ]
    loads = [
        pltpu.make_async_copy(
            tok_hbm.at[z, pl.ds(y * span, span)],
            tok_ref.at[z, pl.ds(y * span, span)],
            sems.at[2 + i],
        )
        for i, (z, y) in enumerate(cuts)
    ]
    for copy in first + loads:
        copy.start()
    for copy in first:
        copy.wait()
    row = start_ref[0] + lax.broadcasted_iota(jnp.int32, (feat, units), 0)
    scale = jnp.broadcast_to(scales_ref[0:1, :], (feat, units))
    for i in range(1, scales_ref.shape[0]):
        scale = jnp.where(row >= i * BLOCK, scales_ref[i : i + 1, :], scale)
    weight = (codes_ref[...].astype(F32) * scale).astype(BF16)
    w_ref[...] = weight
    for (z, y), copy in zip(cuts, loads):
        copy.wait()
        ys = slice(y * span, (y + 1) * span)
        piece = tok_ref[z, ys]
        res = jnp.dot(piece.reshape(-1, feat), weight, preferred_element_type=F32)
        res = res.astype(BF16).reshape(piece.shape[:-1] + (units,))
        for h in range(2):
            out_ref[h, ys, z] = res[:, :, h]


def activate(side_ref, got_ref, cot_ref, far_cot_ref, act_ref, far_act_ref, slope_ref):
    side = side_ref[0]
    for k in range(2):
        which = side if k == 0 else 1 - side
        pre = jnp.sum(got_ref[:, which].astype(F32), axis=0)
        cot = cot_ref[:, side] if k == 0 else far_cot_ref[...]
        cot = cot.reshape(pre.shape).astype(F32)
        square = pre * pre
        tanh = jnp.tanh(ROOT * (pre + 0.044715 * square * pre))
        act = (0.5 * pre * (1.0 + tanh)).astype(BF16)
        if k == 0:
            act_ref[...] = act
        else:
            far_act_ref[...] = act
        inner = ROOT * (1.0 + 3.0 * 0.044715 * square)
        grad = 0.5 * (1.0 + tanh) + 0.5 * pre * (1.0 - tanh * tanh) * inner
        slope_ref[which] = (cot * grad).astype(BF16)


def back(core, slope_ref, w_ref):
    rows = slope_ref[:, :, :, core]
    return lax.dot_general(
        rows.reshape(-1, rows.shape[-1]),
        w_ref[...],
        (((1,), (1,)), ((), ())),
        preferred_element_type=F32,
    )


def back_other(core_ref, slope_ref, w_ref, far_w_ref, out_ref):
    core = 1 - core_ref[0]
    for k, weight in enumerate((w_ref, far_w_ref)):
        out_ref[k] = back(core, slope_ref, weight).astype(BF16)


def back_mine(core_ref, side_ref, slope_ref, w_ref, far_w_ref, other_ref, out_ref):
    core, side = core_ref[0], side_ref[0]
    for k, weight in enumerate((w_ref, far_w_ref)):
        total = back(core, slope_ref, weight) + other_ref[k].astype(F32)
        which = side if k == 0 else 1 - side
        out_ref[which] = total.astype(BF16).reshape(out_ref.shape[1:])


def finish(got_ref, out_ref):
    out_ref[...] = jnp.sum(got_ref[...].astype(F32), axis=1).astype(BF16)


def outer(rows, grads):
    return lax.dot_general(
        rows.reshape(-1, rows.shape[-1]),
        grads.reshape(-1, grads.shape[-1]),
        (((0,), (0,)), ((), ())),
        preferred_element_type=F32,
    )


def weigh_far(far_tok_ref, slope_ref, out_ref):
    total = sum(outer(far_tok_ref[z], slope_ref[:, z]) for z in range(2))
    out_ref[...] = total.astype(BF16)


def weigh_own(factor, side_ref, tok_ref, slope_ref, far_ref, out_ref):
    side = side_ref[0]
    total = sum(outer(tok_ref[z, :, :, side], slope_ref[:, z]) for z in range(2))
    out_ref[...] = (total + far_ref[...].astype(F32)) * factor


def shards(locals_, nodes, tokens, codes, scales, cotangent):
    rows, feat = tokens.shape
    units = codes.shape[1]
    ys = locals_ // 2
    per = nodes // locals_
    sub = rows // nodes // 2
    mine = per * sub
    node = lax.axis_index("node").astype(jnp.int32)
    local = lax.axis_index("local").astype(jnp.int32)
    start = (local * feat).reshape(1)
    core = (node % 2).reshape(1)
    side = (local // ys).reshape(1)
    tok = tokens.reshape(2, ys, per, 2, sub, feat)
    cot = cotangent.reshape(per, 2, sub, units)
    pair = [(i, (i + ys) % locals_) for i in range(locals_)]
    flops = 2 * rows * feat * units
    size = 2 * rows * feat

    weight, partial = pl.pallas_call(
        project,
        out_shape=[
            jax.ShapeDtypeStruct((feat, units), BF16),
            jax.ShapeDtypeStruct((2, ys, 2, per, sub, units), BF16),
        ],
        in_specs=[SMEM, HBM, HBM, HBM],
        out_specs=[VMEM, VMEM],
        scratch_shapes=[
            pltpu.VMEM(tok.shape, BF16),
            pltpu.VMEM(codes.shape, BF16),
            pltpu.VMEM(scales.shape, F32),
            pltpu.SemaphoreType.DMA((6,)),
        ],
        compiler_params=pltpu.CompilerParams(vmem_limit_bytes=58 * 2**20),
        cost_estimate=pl.CostEstimate(flops=flops, bytes_accessed=2 * size, transcendentals=0),
    )(start, tok, codes, scales)
    got = lax.all_to_all(
        partial.reshape(locals_, 2 * mine, units), "local", 0, 0, tiled=True
    ).reshape(locals_, 2, mine, units)
    far_cot = lax.ppermute(
        lax.dynamic_index_in_dim(cot, 1 - side[0], 1, False), "local", pair
    )
    far_weight = lax.ppermute(weight, "local", pair)
    block = nodes // 4
    step = [
        (n * locals_ + l, (n + (block if l >= ys else -block)) % nodes * locals_ + (l + ys) % locals_)
        for n in range(nodes)
        for l in range(locals_)
    ]
    far_tok = lax.ppermute(
        lax.dynamic_index_in_dim(tok, 1 - side[0], 3, False), ("node", "local"), step
    )
    got, far_cot, far_weight, far_tok = lax.optimization_barrier(
        (got, far_cot, far_weight, far_tok)
    )
    act_own, act_far, slope = call(
        activate,
        [((mine, units), BF16), ((mine, units), BF16), ((2, mine, units), BF16)],
        [SMEM, VMEM, VMEM, VMEM],
        rows * units * 4, size,
        side, got, cot, far_cot,
    )
    lines = [list(range(z * ys, (z + 1) * ys)) for z in range(2)]
    spread = lax.all_gather(
        slope.reshape(2 * mine, units), "local", axis=0, tiled=True, axis_index_groups=lines
    )
    by_core = spread.reshape(ys, 2, per // 2, 2, sub, units)
    by_side = spread.reshape(ys, 2, per, sub, units)
    (other,) = call(
        back_other,
        [((2, rows // 4, feat), BF16)],
        [SMEM, VMEM, VMEM, VMEM],
        flops // 2, size,
        core, by_core, weight, far_weight,
    )
    other = lax.ppermute(other, "node", [(i, i ^ 1) for i in range(nodes)])
    (far_part,) = call(
        weigh_far, [((feat, units), BF16)], [VMEM, VMEM], flops // 2, size, far_tok, by_side
    )
    far_part = lax.ppermute(far_part, "local", pair)
    (both,) = call(
        back_mine,
        [((2, ys, 2, per // 2, sub, feat), BF16)],
        [SMEM, SMEM, VMEM, VMEM, VMEM, VMEM],
        flops // 2, size,
        core, side, by_core, weight, far_weight, other,
    )
    groups = [
        [
            (per * (ys * t + y) + 2 * h + c) * locals_ + z * ys + own
            for z in range(2)
            for y in range(ys)
            for t in range(2)
            for h in range(per // 2)
        ]
        for c in range(2)
        for own in range(ys)
    ]
    sums = lax.all_to_all(
        both.reshape(nodes, sub, feat),
        ("node", "local"), 0, 0, axis_index_groups=groups, tiled=True,
    ).reshape(2, nodes // 2, sub, feat)
    (weight_grad,) = call(
        functools.partial(weigh_own, rows ** (-0.5)),
        [((feat, units), F32)],
        [SMEM, VMEM, VMEM, VMEM],
        flops // 2, size,
        side, tok, by_side, far_part,
    )
    (input_grad,) = call(
        finish, [((2, sub, feat), BF16)], [VMEM], rows * feat, size // 2, sums
    )
    act_far = lax.ppermute(act_far, "local", pair)
    first = side[0] == 0
    act_own, act_far = act_own.reshape(per, sub, units), act_far.reshape(per, sub, units)
    act = jnp.stack(
        [jnp.where(first, act_own, act_far), jnp.where(first, act_far, act_own)], axis=1
    )
    return (
        act.reshape(rows // locals_, units),
        input_grad.reshape(rows // nodes, feat),
        weight_grad,
    )


def solution(mesh):
    body = functools.partial(shards, mesh.shape["local"], mesh.shape["node"])
    placed = (P(None, "local"), P("local", "node"), P(None, "node"), P("local", "node"))
    return jax.shard_map(
        lambda *args: body(*args),
        mesh=mesh,
        in_specs=placed,
        out_specs=(P("local", "node"), P("node", "local"), P("local", "node")),
        check_vma=False,
    )
```

```python
import functools
import math

import jax
import jax.numpy as jnp
from jax import lax
from jax.experimental import pallas as pl
from jax.experimental.pallas import tpu as pltpu
from jax.sharding import PartitionSpec as P

BLOCK = 2048
F32 = jnp.float32
BF16 = jnp.bfloat16
ROOT = math.sqrt(2.0 / math.pi)
VMEM = pl.BlockSpec(memory_space=pltpu.VMEM)
SMEM = pl.BlockSpec(memory_space=pltpu.SMEM)


def call(kernel, outs, specs, flops, size, *args):
    return pl.pallas_call(
        kernel,
        out_shape=[jax.ShapeDtypeStruct(s, d) for s, d in outs],
        in_specs=specs,
        out_specs=[VMEM] * len(outs),
        compiler_params=pltpu.CompilerParams(vmem_limit_bytes=40 * 2**20),
        cost_estimate=pl.CostEstimate(flops=flops, bytes_accessed=size, transcendentals=0),
    )(*args)


HBM = pl.BlockSpec(memory_space=pltpu.HBM)


def project(start_ref, tok_hbm, codes_hbm, scales_hbm, w_ref, out_ref, tok_ref, codes_ref, scales_ref, sems):
    feat, units = codes_ref.shape
    cuts = [(z, y) for z in range(2) for y in (0, 1)]
    span = tok_ref.shape[1] // 2
    first = [
        pltpu.make_async_copy(codes_hbm, codes_ref, sems.at[0]),
        pltpu.make_async_copy(scales_hbm, scales_ref, sems.at[1]),
    ]
    loads = [
        pltpu.make_async_copy(
            tok_hbm.at[z, pl.ds(y * span, span)],
            tok_ref.at[z, pl.ds(y * span, span)],
            sems.at[2 + i],
        )
        for i, (z, y) in enumerate(cuts)
    ]
    for copy in first + loads:
        copy.start()
    for copy in first:
        copy.wait()
    row = start_ref[0] + lax.broadcasted_iota(jnp.int32, (feat, units), 0)
    scale = jnp.broadcast_to(scales_ref[0:1, :], (feat, units))
    for i in range(1, scales_ref.shape[0]):
        scale = jnp.where(row >= i * BLOCK, scales_ref[i : i + 1, :], scale)
    weight = (codes_ref[...].astype(F32) * scale).astype(BF16)
    w_ref[...] = weight
    for (z, y), copy in zip(cuts, loads):
        copy.wait()
        ys = slice(y * span, (y + 1) * span)
        piece = tok_ref[z, ys]
        res = jnp.dot(piece.reshape(-1, feat), weight, preferred_element_type=F32)
        res = res.astype(BF16).reshape(piece.shape[:-1] + (units,))
        for h in range(2):
            out_ref[h, ys, z] = res[:, :, h]


def activate(side_ref, got_ref, cot_ref, far_cot_ref, act_ref, far_act_ref, slope_ref):
    side = side_ref[0]
    for k in range(2):
        which = side if k == 0 else 1 - side
        pre = jnp.sum(got_ref[:, which].astype(F32), axis=0)
        cot = cot_ref[:, side] if k == 0 else far_cot_ref[...]
        cot = cot.reshape(pre.shape).astype(F32)
        square = pre * pre
        tanh = jnp.tanh(ROOT * (pre + 0.044715 * square * pre))
        act = (0.5 * pre * (1.0 + tanh)).astype(BF16)
        if k == 0:
            act_ref[...] = act
        else:
            far_act_ref[...] = act
        inner = ROOT * (1.0 + 3.0 * 0.044715 * square)
        grad = 0.5 * (1.0 + tanh) + 0.5 * pre * (1.0 - tanh * tanh) * inner
        slope_ref[which] = (cot * grad).astype(BF16)


def back(core, slope_ref, w_ref):
    rows = slope_ref[:, :, :, core]
    return lax.dot_general(
        rows.reshape(-1, rows.shape[-1]),
        w_ref[...],
        (((1,), (1,)), ((), ())),
        preferred_element_type=F32,
    )


def back_other(core_ref, slope_ref, w_ref, far_w_ref, out_ref):
    core = 1 - core_ref[0]
    for k, weight in enumerate((w_ref, far_w_ref)):
        out_ref[k] = back(core, slope_ref, weight).astype(BF16)


def back_mine(core_ref, side_ref, slope_ref, w_ref, far_w_ref, other_ref, out_ref):
    core, side = core_ref[0], side_ref[0]
    for k, weight in enumerate((w_ref, far_w_ref)):
        total = back(core, slope_ref, weight) + other_ref[k].astype(F32)
        which = side if k == 0 else 1 - side
        out_ref[which] = total.astype(BF16).reshape(out_ref.shape[1:])


def finish(got_ref, out_ref):
    out_ref[...] = jnp.sum(got_ref[...].astype(F32), axis=1).astype(BF16)


def outer(rows, grads):
    return lax.dot_general(
        rows.reshape(-1, rows.shape[-1]),
        grads.reshape(-1, grads.shape[-1]),
        (((0,), (0,)), ((), ())),
        preferred_element_type=F32,
    )


def weigh_far(far_tok_ref, slope_ref, out_ref):
    total = sum(outer(far_tok_ref[z], slope_ref[:, z]) for z in range(2))
    out_ref[...] = total.astype(BF16)


def weigh_own(factor, side_ref, tok_ref, slope_ref, far_ref, out_ref):
    side = side_ref[0]
    total = sum(outer(tok_ref[z, :, :, side], slope_ref[:, z]) for z in range(2))
    out_ref[...] = (total + far_ref[...].astype(F32)) * factor


def shards(locals_, nodes, tokens, codes, scales, cotangent):
    rows, feat = tokens.shape
    units = codes.shape[1]
    ys = locals_ // 2
    per = nodes // locals_
    sub = rows // nodes // 2
    mine = per * sub
    node = lax.axis_index("node").astype(jnp.int32)
    local = lax.axis_index("local").astype(jnp.int32)
    start = (local * feat).reshape(1)
    core = (node % 2).reshape(1)
    side = (local // ys).reshape(1)
    tok = tokens.reshape(2, ys, per, 2, sub, feat)
    cot = cotangent.reshape(per, 2, sub, units)
    pair = [(i, (i + ys) % locals_) for i in range(locals_)]
    flops = 2 * rows * feat * units
    size = 2 * rows * feat

    weight, partial = pl.pallas_call(
        project,
        out_shape=[
            jax.ShapeDtypeStruct((feat, units), BF16),
            jax.ShapeDtypeStruct((2, ys, 2, per, sub, units), BF16),
        ],
        in_specs=[SMEM, HBM, HBM, HBM],
        out_specs=[VMEM, VMEM],
        scratch_shapes=[
            pltpu.VMEM(tok.shape, BF16),
            pltpu.VMEM(codes.shape, BF16),
            pltpu.VMEM(scales.shape, F32),
            pltpu.SemaphoreType.DMA((6,)),
        ],
        compiler_params=pltpu.CompilerParams(vmem_limit_bytes=58 * 2**20),
        cost_estimate=pl.CostEstimate(flops=flops, bytes_accessed=2 * size, transcendentals=0),
    )(start, tok, codes, scales)
    got = lax.all_to_all(
        partial.reshape(locals_, 2 * mine, units), "local", 0, 0, tiled=True
    ).reshape(locals_, 2, mine, units)
    far_cot = lax.ppermute(
        lax.dynamic_index_in_dim(cot, 1 - side[0], 1, False), "local", pair
    )
    far_weight = lax.ppermute(weight, "local", pair)
    block = nodes // 4
    step = [
        (n * locals_ + l, (n + (block if l >= ys else -block)) % nodes * locals_ + (l + ys) % locals_)
        for n in range(nodes)
        for l in range(locals_)
    ]
    far_tok = lax.ppermute(
        lax.dynamic_index_in_dim(tok, 1 - side[0], 3, False), ("node", "local"), step
    )
    got, far_cot, far_weight, far_tok = lax.optimization_barrier(
        (got, far_cot, far_weight, far_tok)
    )
    act_own, act_far, slope = call(
        activate,
        [((mine, units), BF16), ((mine, units), BF16), ((2, mine, units), BF16)],
        [SMEM, VMEM, VMEM, VMEM],
        rows * units * 4, size,
        side, got, cot, far_cot,
    )
    lines = [list(range(z * ys, (z + 1) * ys)) for z in range(2)]
    spread = lax.all_gather(
        slope.reshape(2 * mine, units), "local", axis=0, tiled=True, axis_index_groups=lines
    )
    by_core = spread.reshape(ys, 2, per // 2, 2, sub, units)
    by_side = spread.reshape(ys, 2, per, sub, units)
    (other,) = call(
        back_other,
        [((2, rows // 4, feat), BF16)],
        [SMEM, VMEM, VMEM, VMEM],
        flops // 2, size,
        core, by_core, weight, far_weight,
    )
    other = lax.ppermute(other, "node", [(i, i ^ 1) for i in range(nodes)])
    (far_part,) = call(
        weigh_far, [((feat, units), BF16)], [VMEM, VMEM], flops // 2, size, far_tok, by_side
    )
    far_part = lax.ppermute(far_part, "local", pair)
    (both,) = call(
        back_mine,
        [((2, ys, 2, per // 2, sub, feat), BF16)],
        [SMEM, SMEM, VMEM, VMEM, VMEM, VMEM],
        flops // 2, size,
        core, side, by_core, weight, far_weight, other,
    )
    both, act_far = lax.optimization_barrier((both, act_far))
    groups = [
        [
            (per * (ys * t + y) + 2 * h + c) * locals_ + z * ys + own
            for z in range(2)
            for y in range(ys)
            for t in range(2)
            for h in range(per // 2)
        ]
        for c in range(2)
        for own in range(ys)
    ]
    sums = lax.all_to_all(
        both.reshape(nodes, sub, feat),
        ("node", "local"), 0, 0, axis_index_groups=groups, tiled=True,
    ).reshape(2, nodes // 2, sub, feat)
    (weight_grad,) = call(
        functools.partial(weigh_own, rows ** (-0.5)),
        [((feat, units), F32)],
        [SMEM, VMEM, VMEM, VMEM],
        20 * flops, size,
        side, tok, by_side, far_part,
    )
    (input_grad,) = call(
        finish, [((2, sub, feat), BF16)], [VMEM], rows * feat, size // 2, sums
    )
    act_far = lax.ppermute(act_far, "local", pair)
    first = side[0] == 0
    act_own, act_far = act_own.reshape(per, sub, units), act_far.reshape(per, sub, units)
    act = jnp.stack(
        [jnp.where(first, act_own, act_far), jnp.where(first, act_far, act_own)], axis=1
    )
    return (
        act.reshape(rows // locals_, units),
        input_grad.reshape(rows // nodes, feat),
        weight_grad,
    )


def solution(mesh):
    body = functools.partial(shards, mesh.shape["local"], mesh.shape["node"])
    placed = (P(None, "local"), P("local", "node"), P(None, "node"), P("local", "node"))
    return jax.shard_map(
        lambda *args: body(*args),
        mesh=mesh,
        in_specs=placed,
        out_specs=(P("local", "node"), P("node", "local"), P("local", "node")),
        check_vma=False,
    )
```

```python
import functools
import math

import jax
import jax.numpy as jnp
from jax import lax
from jax.experimental import pallas as pl
from jax.experimental.pallas import tpu as pltpu
from jax.sharding import PartitionSpec as P

BLOCK = 2048
F32 = jnp.float32
BF16 = jnp.bfloat16
ROOT = math.sqrt(2.0 / math.pi)
VMEM = pl.BlockSpec(memory_space=pltpu.VMEM)
SMEM = pl.BlockSpec(memory_space=pltpu.SMEM)


def call(kernel, outs, specs, flops, size, *args, room=40):
    return pl.pallas_call(
        kernel,
        out_shape=[jax.ShapeDtypeStruct(s, d) for s, d in outs],
        in_specs=specs,
        out_specs=[VMEM] * len(outs),
        compiler_params=pltpu.CompilerParams(vmem_limit_bytes=room * 2**20),
        cost_estimate=pl.CostEstimate(flops=flops, bytes_accessed=size, transcendentals=0),
    )(*args)


HBM = pl.BlockSpec(memory_space=pltpu.HBM)


def dequant(start_ref, codes, scales_ref):
    row = start_ref[0] + lax.broadcasted_iota(jnp.int32, codes.shape, 0)
    scale = jnp.broadcast_to(scales_ref[0:1, :], codes.shape)
    for i in range(1, scales_ref.shape[0]):
        scale = jnp.where(row >= i * BLOCK, scales_ref[i : i + 1, :], scale)
    return (codes.astype(F32) * scale).astype(BF16)


def project_own(start_ref, side_ref, tok_hbm, codes_hbm, scales_hbm, w_ref, out_ref, tok_ref, codes_ref, scales_ref, sems):
    side = side_ref[0]
    first = [
        pltpu.make_async_copy(codes_hbm, codes_ref, sems.at[0]),
        pltpu.make_async_copy(scales_hbm, scales_ref, sems.at[1]),
    ]
    loads = [
        pltpu.make_async_copy(tok_hbm.at[z, :, :, side], tok_ref.at[z], sems.at[2 + z])
        for z in range(2)
    ]
    for copy in first + loads:
        copy.start()
    for copy in first:
        copy.wait()
    weight = dequant(start_ref, codes_ref[...], scales_ref)
    w_ref[...] = weight
    for z, copy in enumerate(loads):
        copy.wait()
        rows = tok_ref[z].reshape(-1, tok_ref.shape[-1])
        res = jnp.dot(rows, weight, preferred_element_type=F32)
        out_ref[z] = res.reshape(out_ref.shape[1:])


def project_far(start_ref, codes_ref, scales_ref, tok_a_ref, tok_b_ref, own_ref, w_ref, out_ref):
    weight = dequant(start_ref, codes_ref[...], scales_ref)
    w_ref[...] = weight
    for z in range(2):
        low = 0
        for tok in (tok_a_ref, tok_b_ref):
            high = low + tok.shape[1]
            rows = tok[z].reshape(-1, tok.shape[-1])
            res = jnp.dot(rows, weight, preferred_element_type=F32)
            both = res.reshape((high - low,) + out_ref.shape[2:]) + own_ref[z, low:high]
            out_ref[low:high, z] = both.astype(BF16)
            low = high


def activate(side_ref, got_ref, cot_ref, far_cot_ref, act_ref, far_act_ref, slope_ref):
    side = side_ref[0]
    for k in range(2):
        which = side if k == 0 else 1 - side
        pre = jnp.sum(got_ref[:, which].astype(F32), axis=0)
        cot = cot_ref[:, side] if k == 0 else far_cot_ref[...]
        cot = cot.reshape(pre.shape).astype(F32)
        square = pre * pre
        tanh = jnp.tanh(ROOT * (pre + 0.044715 * square * pre))
        act = (0.5 * pre * (1.0 + tanh)).astype(BF16)
        if k == 0:
            act_ref[...] = act
        else:
            far_act_ref[...] = act
        inner = ROOT * (1.0 + 3.0 * 0.044715 * square)
        grad = 0.5 * (1.0 + tanh) + 0.5 * pre * (1.0 - tanh * tanh) * inner
        slope_ref[which] = (cot * grad).astype(BF16)


def back(core, slope_ref, w_ref):
    rows = slope_ref[:, :, :, core]
    return lax.dot_general(
        rows.reshape(-1, rows.shape[-1]),
        w_ref[...],
        (((1,), (1,)), ((), ())),
        preferred_element_type=F32,
    )


def back_other(core_ref, slope_ref, w_ref, far_w_ref, out_ref):
    core = 1 - core_ref[0]
    for k, weight in enumerate((w_ref, far_w_ref)):
        out_ref[k] = back(core, slope_ref, weight).astype(BF16)


def back_mine(core_ref, side_ref, slope_ref, w_ref, far_w_ref, other_ref, out_ref):
    core, side = core_ref[0], side_ref[0]
    for k, weight in enumerate((w_ref, far_w_ref)):
        total = back(core, slope_ref, weight) + other_ref[k].astype(F32)
        which = side if k == 0 else 1 - side
        out_ref[which] = total.astype(BF16).reshape(out_ref.shape[1:])


def finish(got_ref, out_ref):
    out_ref[...] = jnp.sum(got_ref[...].astype(F32), axis=1).astype(BF16)


def outer(rows, grads):
    return lax.dot_general(
        rows.reshape(-1, rows.shape[-1]),
        grads.reshape(-1, grads.shape[-1]),
        (((0,), (0,)), ((), ())),
        preferred_element_type=F32,
    )


def weigh_far(tok_a_ref, tok_b_ref, slope_ref, out_ref):
    total = None
    for z in range(2):
        low = 0
        for tok in (tok_a_ref, tok_b_ref):
            high = low + tok.shape[1]
            part = outer(tok[z], slope_ref[low:high, z])
            total = part if total is None else total + part
            low = high
    out_ref[...] = total.astype(BF16)


def weigh_own(factor, side_ref, tok_ref, slope_ref, far_ref, out_ref):
    side = side_ref[0]
    total = sum(outer(tok_ref[z, :, :, side], slope_ref[:, z]) for z in range(2))
    out_ref[...] = (total + far_ref[...].astype(F32)) * factor


def shards(locals_, nodes, tokens, codes, scales, cotangent):
    rows, feat = tokens.shape
    units = codes.shape[1]
    ys = locals_ // 2
    per = nodes // locals_
    sub = rows // nodes // 2
    mine = per * sub
    node = lax.axis_index("node").astype(jnp.int32)
    local = lax.axis_index("local").astype(jnp.int32)
    start = (local * feat).reshape(1)
    core = (node % 2).reshape(1)
    side = (local // ys).reshape(1)
    tok = tokens.reshape(2, ys, per, 2, sub, feat)
    cot = cotangent.reshape(per, 2, sub, units)
    pair = [(i, (i + ys) % locals_) for i in range(locals_)]
    flops = 2 * rows * feat * units
    size = 2 * rows * feat

    far_codes = lax.ppermute(codes, "local", pair)
    leave = lax.dynamic_index_in_dim(tok, 1 - side[0], 3, False)
    cut = (3 * ys) // 4
    block = nodes // 4
    step = [
        (n * locals_ + l, (n + (block if l >= ys else -block)) % nodes * locals_ + (l + ys) % locals_)
        for n in range(nodes)
        for l in range(locals_)
    ]
    far_tok_a = lax.ppermute(leave[:, :cut], ("node", "local"), step)
    far_tok_b = lax.ppermute(leave[:, cut:], "local", pair)
    far_start = ((local + ys) % locals_ * feat).reshape(1)
    weight, own = pl.pallas_call(
        project_own,
        out_shape=[
            jax.ShapeDtypeStruct((feat, units), BF16),
            jax.ShapeDtypeStruct((2, ys, mine, units), F32),
        ],
        in_specs=[SMEM, SMEM, HBM, HBM, HBM],
        out_specs=[VMEM, VMEM],
        scratch_shapes=[
            pltpu.VMEM((2, ys, per, sub, feat), BF16),
            pltpu.VMEM(codes.shape, BF16),
            pltpu.VMEM(scales.shape, F32),
            pltpu.SemaphoreType.DMA((4,)),
        ],
        compiler_params=pltpu.CompilerParams(vmem_limit_bytes=40 * 2**20),
        cost_estimate=pl.CostEstimate(flops=flops // 2, bytes_accessed=size, transcendentals=0),
    )(start, side, tok, codes, scales)
    far_weight, partial = call(
        project_far,
        [((feat, units), BF16), ((ys, 2, mine, units), BF16)],
        [SMEM] + [VMEM] * 5,
        flops // 2, size,
        far_start, far_codes, scales, far_tok_a, far_tok_b, own, room=40,
    )
    lines = [list(range(z * ys, (z + 1) * ys)) for z in range(2)]
    got = lax.all_to_all(
        partial.reshape(ys, 2 * mine, units), "local", 0, 0, axis_index_groups=lines, tiled=True
    ).reshape(ys, 2, mine, units)
    far_cot = lax.ppermute(
        lax.dynamic_index_in_dim(cot, 1 - side[0], 1, False), "local", pair
    )
    act_own, act_far, slope = call(
        activate,
        [((mine, units), BF16), ((mine, units), BF16), ((2, mine, units), BF16)],
        [SMEM, VMEM, VMEM, VMEM],
        rows * units * 4, size,
        side, got, cot, far_cot,
    )
    spread = lax.all_gather(
        slope.reshape(2 * mine, units), "local", axis=0, tiled=True, axis_index_groups=lines
    )
    by_core = spread.reshape(ys, 2, per // 2, 2, sub, units)
    by_side = spread.reshape(ys, 2, per, sub, units)
    (other,) = call(
        back_other,
        [((2, rows // 4, feat), BF16)],
        [SMEM, VMEM, VMEM, VMEM],
        flops // 2, size,
        core, by_core, weight, far_weight,
    )
    other = lax.ppermute(other, "node", [(i, i ^ 1) for i in range(nodes)])
    (far_part,) = call(
        weigh_far, [((feat, units), BF16)], [VMEM] * 3, flops // 2, size,
        far_tok_a, far_tok_b, by_side,
    )
    far_part = lax.ppermute(far_part, "local", pair)
    (both,) = call(
        back_mine,
        [((2, ys, 2, per // 2, sub, feat), BF16)],
        [SMEM, SMEM, VMEM, VMEM, VMEM, VMEM],
        flops // 2, size,
        core, side, by_core, weight, far_weight, other, room=40,
    )
    both, act_far = lax.optimization_barrier((both, act_far))
    groups = [
        [
            (per * (ys * t + y) + 2 * h + c) * locals_ + z * ys + own
            for z in range(2)
            for y in range(ys)
            for t in range(2)
            for h in range(per // 2)
        ]
        for c in range(2)
        for own in range(ys)
    ]
    sums = lax.all_to_all(
        both.reshape(nodes, sub, feat),
        ("node", "local"), 0, 0, axis_index_groups=groups, tiled=True,
    ).reshape(2, nodes // 2, sub, feat)
    (weight_grad,) = call(
        functools.partial(weigh_own, rows ** (-0.5)),
        [((feat, units), F32)],
        [SMEM, VMEM, VMEM, VMEM],
        20 * flops, size,
        side, tok, by_side, far_part,
    )
    (input_grad,) = call(
        finish, [((2, sub, feat), BF16)], [VMEM], rows * feat, size // 2, sums
    )
    act_far = lax.ppermute(act_far, "local", pair)
    first = side[0] == 0
    act_own, act_far = act_own.reshape(per, sub, units), act_far.reshape(per, sub, units)
    act = jnp.stack(
        [jnp.where(first, act_own, act_far), jnp.where(first, act_far, act_own)], axis=1
    )
    return (
        act.reshape(rows // locals_, units),
        input_grad.reshape(rows // nodes, feat),
        weight_grad,
    )


def solution(mesh):
    body = functools.partial(shards, mesh.shape["local"], mesh.shape["node"])
    placed = (P(None, "local"), P("local", "node"), P(None, "node"), P("local", "node"))
    return jax.shard_map(
        lambda *args: body(*args),
        mesh=mesh,
        in_specs=placed,
        out_specs=(P("local", "node"), P("node", "local"), P("local", "node")),
        check_vma=False,
    )
```

```python
import functools
import math

import jax
import jax.numpy as jnp
from jax import lax
from jax.experimental import pallas as pl
from jax.experimental.pallas import tpu as pltpu
from jax.sharding import PartitionSpec as P

BLOCK = 2048
F32 = jnp.float32
BF16 = jnp.bfloat16
ROOT = math.sqrt(2.0 / math.pi)
VMEM = pl.BlockSpec(memory_space=pltpu.VMEM)
SMEM = pl.BlockSpec(memory_space=pltpu.SMEM)


def call(kernel, outs, specs, flops, size, *args):
    return pl.pallas_call(
        kernel,
        out_shape=[jax.ShapeDtypeStruct(s, d) for s, d in outs],
        in_specs=specs,
        out_specs=[VMEM] * len(outs),
        compiler_params=pltpu.CompilerParams(vmem_limit_bytes=40 * 2**20),
        cost_estimate=pl.CostEstimate(flops=flops, bytes_accessed=size, transcendentals=0),
    )(*args)


HBM = pl.BlockSpec(memory_space=pltpu.HBM)


def project(start_ref, tok_hbm, codes_hbm, scales_hbm, w_ref, out_hbm, tok_ref, codes_ref, scales_ref, out_ref, sems):
    feat, units = codes_ref.shape
    cuts = [(z, y) for z in range(2) for y in (0, 1)]
    span = tok_ref.shape[1] // 2
    first = [
        pltpu.make_async_copy(codes_hbm, codes_ref, sems.at[0]),
        pltpu.make_async_copy(scales_hbm, scales_ref, sems.at[1]),
    ]
    loads = [
        pltpu.make_async_copy(
            tok_hbm.at[z, pl.ds(y * span, span)],
            tok_ref.at[z, pl.ds(y * span, span)],
            sems.at[2 + i],
        )
        for i, (z, y) in enumerate(cuts)
    ]
    for copy in first + loads:
        copy.start()
    for copy in first:
        copy.wait()
    row = start_ref[0] + lax.broadcasted_iota(jnp.int32, (feat, units), 0)
    scale = jnp.broadcast_to(scales_ref[0:1, :], (feat, units))
    for i in range(1, scales_ref.shape[0]):
        scale = jnp.where(row >= i * BLOCK, scales_ref[i : i + 1, :], scale)
    weight = (codes_ref[...].astype(F32) * scale).astype(BF16)
    w_ref[...] = weight
    stores = []
    for i, ((z, y), copy) in enumerate(zip(cuts, loads)):
        copy.wait()
        ys = slice(y * span, (y + 1) * span)
        piece = tok_ref[z, ys]
        res = jnp.dot(piece.reshape(-1, feat), weight, preferred_element_type=F32)
        res = res.astype(BF16).reshape(piece.shape[:-1] + (units,))
        for h in range(2):
            out_ref[h, ys, z] = res[:, :, h]
        part = pl.ds(y * span, span)
        store = pltpu.make_async_copy(
            out_ref.at[:, part, z], out_hbm.at[:, part, z], sems.at[6 + i]
        )
        store.start()
        stores.append(store)
    for store in stores:
        store.wait()


def activate(side_ref, got_ref, cot_ref, far_cot_ref, act_ref, far_act_ref, slope_ref):
    side = side_ref[0]
    for k in range(2):
        which = side if k == 0 else 1 - side
        pre = jnp.sum(got_ref[:, which].astype(F32), axis=0)
        cot = cot_ref[:, side] if k == 0 else far_cot_ref[...]
        cot = cot.reshape(pre.shape).astype(F32)
        square = pre * pre
        tanh = jnp.tanh(ROOT * (pre + 0.044715 * square * pre))
        act = (0.5 * pre * (1.0 + tanh)).astype(BF16)
        if k == 0:
            act_ref[...] = act
        else:
            far_act_ref[...] = act
        inner = ROOT * (1.0 + 3.0 * 0.044715 * square)
        grad = 0.5 * (1.0 + tanh) + 0.5 * pre * (1.0 - tanh * tanh) * inner
        slope_ref[which] = (cot * grad).astype(BF16)


def back(core, slope_ref, w_ref):
    rows = slope_ref[:, :, :, core]
    return lax.dot_general(
        rows.reshape(-1, rows.shape[-1]),
        w_ref[...],
        (((1,), (1,)), ((), ())),
        preferred_element_type=F32,
    )


def back_other(core_ref, slope_ref, w_ref, far_w_ref, out_ref):
    core = 1 - core_ref[0]
    for k, weight in enumerate((w_ref, far_w_ref)):
        out_ref[k] = back(core, slope_ref, weight).astype(BF16)


def back_mine(core_ref, side_ref, slope_ref, w_ref, far_w_ref, other_ref, out_ref):
    core, side = core_ref[0], side_ref[0]
    for k, weight in enumerate((w_ref, far_w_ref)):
        total = back(core, slope_ref, weight) + other_ref[k].astype(F32)
        which = side if k == 0 else 1 - side
        high, mid, _, wide, low, rows, feat = out_ref.shape
        total = total.astype(BF16).reshape(mid, wide, high, low, rows, feat)
        for t in range(high):
            out_ref[t, :, which] = total[:, :, t]


def finish(got_ref, out_ref):
    for k in range(2):
        part = got_ref[:, k].astype(F32)
        out_ref[k] = jnp.sum(part.reshape((-1,) + part.shape[2:]), axis=0).astype(BF16)


def outer(rows, grads):
    return lax.dot_general(
        rows.reshape(-1, rows.shape[-1]),
        grads.reshape(-1, grads.shape[-1]),
        (((0,), (0,)), ((), ())),
        preferred_element_type=F32,
    )


def weigh_far(far_tok_ref, slope_ref, out_ref):
    total = sum(outer(far_tok_ref[z], slope_ref[:, z]) for z in range(2))
    out_ref[...] = total.astype(BF16)


def weigh_own(factor, side_ref, tok_ref, slope_ref, far_ref, out_ref):
    side = side_ref[0]
    total = sum(outer(tok_ref[z, :, :, side], slope_ref[:, z]) for z in range(2))
    out_ref[...] = (total + far_ref[...].astype(F32)) * factor


def shards(locals_, nodes, tokens, codes, scales, cotangent):
    rows, feat = tokens.shape
    units = codes.shape[1]
    ys = locals_ // 2
    per = nodes // locals_
    sub = rows // nodes // 2
    mine = per * sub
    node = lax.axis_index("node").astype(jnp.int32)
    local = lax.axis_index("local").astype(jnp.int32)
    start = (local * feat).reshape(1)
    core = (node % 2).reshape(1)
    side = (local // ys).reshape(1)
    tok = tokens.reshape(2, ys, per, 2, sub, feat)
    cot = cotangent.reshape(per, 2, sub, units)
    pair = [(i, (i + ys) % locals_) for i in range(locals_)]
    flops = 2 * rows * feat * units
    size = 2 * rows * feat

    weight, partial = pl.pallas_call(
        project,
        out_shape=[
            jax.ShapeDtypeStruct((feat, units), BF16),
            jax.ShapeDtypeStruct((2, ys, 2, per, sub, units), BF16),
        ],
        in_specs=[SMEM, HBM, HBM, HBM],
        out_specs=[VMEM, HBM],
        scratch_shapes=[
            pltpu.VMEM(tok.shape, BF16),
            pltpu.VMEM(codes.shape, BF16),
            pltpu.VMEM(scales.shape, F32),
            pltpu.VMEM((2, ys, 2, per, sub, units), BF16),
            pltpu.SemaphoreType.DMA((10,)),
        ],
        compiler_params=pltpu.CompilerParams(vmem_limit_bytes=58 * 2**20),
        cost_estimate=pl.CostEstimate(flops=flops, bytes_accessed=2 * size, transcendentals=0),
    )(start, tok, codes, scales)
    got = lax.all_to_all(
        partial.reshape(locals_, 2 * mine, units), "local", 0, 0, tiled=True
    ).reshape(locals_, 2, mine, units)
    far_cot = lax.ppermute(
        lax.dynamic_index_in_dim(cot, 1 - side[0], 1, False), "local", pair
    )
    far_weight = lax.ppermute(weight, "local", pair)
    block = nodes // 4
    step = [
        (n * locals_ + l, (n + (block if l >= ys else -block)) % nodes * locals_ + (l + ys) % locals_)
        for n in range(nodes)
        for l in range(locals_)
    ]
    far_tok = lax.ppermute(
        lax.dynamic_index_in_dim(tok, 1 - side[0], 3, False), ("node", "local"), step
    )
    got, far_cot, far_weight, far_tok = lax.optimization_barrier(
        (got, far_cot, far_weight, far_tok)
    )
    act_own, act_far, slope = call(
        activate,
        [((mine, units), BF16), ((mine, units), BF16), ((2, mine, units), BF16)],
        [SMEM, VMEM, VMEM, VMEM],
        rows * units * 4, size,
        side, got, cot, far_cot,
    )
    lines = [list(range(z * ys, (z + 1) * ys)) for z in range(2)]
    spread = lax.all_gather(
        slope.reshape(2 * mine, units), "local", axis=0, tiled=True, axis_index_groups=lines
    )
    by_core = spread.reshape(ys, 2, per // 2, 2, sub, units)
    by_side = spread.reshape(ys, 2, per, sub, units)
    (other,) = call(
        back_other,
        [((2, rows // 4, feat), BF16)],
        [SMEM, VMEM, VMEM, VMEM],
        flops // 2, size,
        core, by_core, weight, far_weight,
    )
    other = lax.ppermute(other, "node", [(i, i ^ 1) for i in range(nodes)])
    (far_part,) = call(
        weigh_far, [((feat, units), BF16)], [VMEM, VMEM], flops // 2, size, far_tok, by_side
    )
    far_part = lax.ppermute(far_part, "local", pair)
    (both,) = call(
        back_mine,
        [((2, 2, 2, ys // 2, per // 2, sub, feat), BF16)],
        [SMEM, SMEM, VMEM, VMEM, VMEM, VMEM],
        flops // 2, size,
        core, side, by_core, weight, far_weight, other,
    )
    both, act_far = lax.optimization_barrier((both, act_far))
    groups = [
        [
            (per * (ys * t + y) + 2 * h + c) * locals_ + z * ys + own
            for t in range(2)
            for m in range(2)
            for z in range(2)
            for y in range(m * ys // 2, (m + 1) * ys // 2)
            for h in range(per // 2)
        ]
        for c in range(2)
        for own in range(ys)
    ]
    sums = lax.all_to_all(
        both.reshape(nodes, sub, feat),
        ("node", "local"), 0, 0, axis_index_groups=groups, tiled=True,
    ).reshape(4, 2, nodes // 8, sub, feat)
    (weight_grad,) = call(
        functools.partial(weigh_own, rows ** (-0.5)),
        [((feat, units), F32)],
        [SMEM, VMEM, VMEM, VMEM],
        20 * flops, size,
        side, tok, by_side, far_part,
    )
    (input_grad,) = call(
        finish, [((2, sub, feat), BF16)], [VMEM], rows * feat, size // 2, sums
    )
    act_far = lax.ppermute(act_far, "local", pair)
    first = side[0] == 0
    act_own, act_far = act_own.reshape(per, sub, units), act_far.reshape(per, sub, units)
    act = jnp.stack(
        [jnp.where(first, act_own, act_far), jnp.where(first, act_far, act_own)], axis=1
    )
    return (
        act.reshape(rows // locals_, units),
        input_grad.reshape(rows // nodes, feat),
        weight_grad,
    )


def solution(mesh):
    body = functools.partial(shards, mesh.shape["local"], mesh.shape["node"])
    placed = (P(None, "local"), P("local", "node"), P(None, "node"), P("local", "node"))
    return jax.shard_map(
        lambda *args: body(*args),
        mesh=mesh,
        in_specs=placed,
        out_specs=(P("local", "node"), P("node", "local"), P("local", "node")),
        check_vma=False,
    )
```

```python
import functools
import math

import jax
import jax.numpy as jnp
from jax import lax
from jax.experimental import pallas as pl
from jax.experimental.pallas import tpu as pltpu
from jax.sharding import PartitionSpec as P

BLOCK = 2048
F32 = jnp.float32
BF16 = jnp.bfloat16
ROOT = math.sqrt(2.0 / math.pi)
VMEM = pl.BlockSpec(memory_space=pltpu.VMEM)
SMEM = pl.BlockSpec(memory_space=pltpu.SMEM)


def call(kernel, outs, specs, flops, size, *args):
    return pl.pallas_call(
        kernel,
        out_shape=[jax.ShapeDtypeStruct(s, d) for s, d in outs],
        in_specs=specs,
        out_specs=[VMEM] * len(outs),
        compiler_params=pltpu.CompilerParams(vmem_limit_bytes=40 * 2**20),
        cost_estimate=pl.CostEstimate(flops=flops, bytes_accessed=size, transcendentals=0),
    )(*args)


HBM = pl.BlockSpec(memory_space=pltpu.HBM)


def project(start_ref, tok_hbm, codes_hbm, scales_hbm, w_ref, out_hbm, tok_ref, codes_ref, scales_ref, out_ref, sems):
    feat, units = codes_ref.shape
    cuts = [(z, y) for z in range(2) for y in (0, 1)]
    span = tok_ref.shape[1] // 2
    first = [
        pltpu.make_async_copy(codes_hbm, codes_ref, sems.at[0]),
        pltpu.make_async_copy(scales_hbm, scales_ref, sems.at[1]),
    ]
    loads = [
        pltpu.make_async_copy(
            tok_hbm.at[z, pl.ds(y * span, span)],
            tok_ref.at[z, pl.ds(y * span, span)],
            sems.at[2 + i],
        )
        for i, (z, y) in enumerate(cuts)
    ]
    for copy in first + loads:
        copy.start()
    for copy in first:
        copy.wait()
    row = start_ref[0] + lax.broadcasted_iota(jnp.int32, (feat, units), 0)
    scale = jnp.broadcast_to(scales_ref[0:1, :], (feat, units))
    for i in range(1, scales_ref.shape[0]):
        scale = jnp.where(row >= i * BLOCK, scales_ref[i : i + 1, :], scale)
    weight = (codes_ref[...].astype(F32) * scale).astype(BF16)
    w_ref[...] = weight
    stores = []
    for i, ((z, y), copy) in enumerate(zip(cuts, loads)):
        copy.wait()
        ys = slice(y * span, (y + 1) * span)
        piece = tok_ref[z, ys]
        res = jnp.dot(piece.reshape(-1, feat), weight, preferred_element_type=F32)
        res = res.astype(BF16).reshape(piece.shape[:-1] + (units,))
        for q in range(2):
            for h in range(2):
                out_ref[q, h, ys, z] = res[:, q, :, h]
        part = pl.ds(y * span, span)
        store = pltpu.make_async_copy(
            out_ref.at[:, :, part, z], out_hbm.at[:, :, part, z], sems.at[6 + i]
        )
        store.start()
        stores.append(store)
    for store in stores:
        store.wait()


def activate(feat, par_ref, side_ref, got_ref, *refs):
    cots, acts, slope_ref = refs[:4], refs[4:8], refs[8]
    par, side = par_ref[0], side_ref[0]
    for i in range(4):
        unit, half = i % 2, i // 2
        q = par if unit == 0 else 1 - par
        t = side if half == 0 else 1 - side
        pre = jnp.sum(got_ref[q, :, t].astype(F32), axis=0)
        cot = cots[i][par, :, side] if i == 0 else cots[i][feat:, :]
        cot = cot.reshape(pre.shape).astype(F32)
        square = pre * pre
        tanh = jnp.tanh(ROOT * (pre + 0.044715 * square * pre))
        acts[i][...] = (0.5 * pre * (1.0 + tanh)).astype(BF16)
        inner = ROOT * (1.0 + 3.0 * 0.044715 * square)
        grad = 0.5 * (1.0 + tanh) + 0.5 * pre * (1.0 - tanh * tanh) * inner
        slope_ref[unit, t] = (cot * grad).astype(BF16)


def gather(par_ref, side_ref, own_ref, x_ref, z_ref, both_ref, out_ref):
    par, side = par_ref[0], side_ref[0]
    for i, ref in enumerate((own_ref, x_ref, z_ref, both_ref)):
        q = par if i % 2 == 0 else 1 - par
        t = side if i < 2 else 1 - side
        out_ref[q, :, t] = ref[...].reshape(out_ref.shape[1], *out_ref.shape[3:])


def back(core, slope_ref, weights, out_feat):
    total = None
    for unit, weight in enumerate(weights):
        rows = slope_ref[:, unit, :, core]
        part = lax.dot_general(
            rows.reshape(-1, rows.shape[-1]),
            weight[: out_feat, :],
            (((1,), (1,)), ((), ())),
            preferred_element_type=F32,
        )
        total = part if total is None else total + part
    return total


def back_other(core_ref, slope_ref, *refs):
    core, out_ref = 1 - core_ref[0], refs[4]
    for k in range(2):
        out_ref[k] = back(
            core, slope_ref, refs[2 * k : 2 * k + 2], out_ref.shape[-1]
        ).astype(BF16)


def back_mine(core_ref, side_ref, slope_ref, *refs):
    core, side = core_ref[0], side_ref[0]
    other_ref, out_ref = refs[4:]
    high, mid, _, wide, rows, feat = out_ref.shape
    for k in range(2):
        total = back(core, slope_ref, refs[2 * k : 2 * k + 2], feat)
        total = total + other_ref[k].astype(F32)
        which = side if k == 0 else 1 - side
        total = total.astype(BF16).reshape(mid, wide, high, rows, feat)
        for t in range(high):
            out_ref[t, :, which] = total[:, :, t]


def finish(got_ref, out_ref):
    for k in range(2):
        part = got_ref[:, k].astype(F32)
        out_ref[k] = jnp.sum(part.reshape((-1,) + part.shape[2:]), axis=0).astype(BF16)


def outer(toks, slope_ref, unit):
    total = None
    for z, rows in enumerate(toks):
        grads = slope_ref[:, unit, z]
        part = lax.dot_general(
            rows.reshape(-1, rows.shape[-1]),
            grads.reshape(-1, grads.shape[-1]),
            (((0,), (0,)), ((), ())),
            preferred_element_type=F32,
        )
        total = part if total is None else total + part
    return total


def weigh_far(par_ref, side_ref, tok_ref, far_tok_ref, slope_ref, x_ref, z_ref, both_ref):
    par, side = par_ref[0], side_ref[0]
    mine = [tok_ref[z, :, par, :, side] for z in range(2)]
    far = [far_tok_ref[z] for z in range(2)]
    z_ref[...] = outer(far, slope_ref, 0).astype(BF16)
    both_ref[...] = outer(far, slope_ref, 1).astype(BF16)
    x_ref[...] = outer(mine, slope_ref, 1).astype(BF16)


def weigh_own(factor, par_ref, side_ref, tok_ref, slope_ref, x_ref, z_ref, both_ref, out_ref):
    par, side = par_ref[0], side_ref[0]
    total = outer([tok_ref[z, :, par, :, side] for z in range(2)], slope_ref, 0)
    for ref in (x_ref, z_ref, both_ref):
        total = total + ref[...].astype(F32)
    out_ref[...] = total * factor


def shards(locals_, nodes, tokens, codes, scales, cotangent):
    rows, feat = tokens.shape
    units = codes.shape[1]
    ys = locals_ // 2
    per = nodes // locals_
    sub = rows // nodes // 2
    mine = 2 * sub
    node = lax.axis_index("node").astype(jnp.int32)
    local = lax.axis_index("local").astype(jnp.int32)
    start = (local * feat).reshape(1)
    core = (node % 2).reshape(1)
    par = (node // 2 % 2).reshape(1)
    side = (local // ys).reshape(1)
    tok = tokens.reshape(2, ys, 2, 2, 2, sub, feat)
    cot = cotangent.reshape(2, 2, 2, sub, units)
    flops = 2 * rows * feat * units
    size = 2 * rows * feat

    def moved(n, l):
        return n % nodes * locals_ + l

    spots = [(n, l) for n in range(nodes) for l in range(locals_)]
    over_x = [(i, i ^ 2) for i in range(nodes)]
    over_z = [(i, (i + ys) % locals_) for i in range(locals_)]
    over_both = [(moved(n, l), moved(n ^ 2, (l + ys) % locals_)) for n, l in spots]

    def send(x, z, both):
        return (
            lax.ppermute(x, "node", over_x),
            lax.ppermute(z, "local", over_z),
            lax.ppermute(both, ("node", "local"), over_both),
        )

    weight, partial = pl.pallas_call(
        project,
        out_shape=[
            jax.ShapeDtypeStruct((feat, units), BF16),
            jax.ShapeDtypeStruct((2, 2, ys, 2, 2, sub, units), BF16),
        ],
        in_specs=[SMEM, HBM, HBM, HBM],
        out_specs=[VMEM, HBM],
        scratch_shapes=[
            pltpu.VMEM(tok.shape, BF16),
            pltpu.VMEM(codes.shape, BF16),
            pltpu.VMEM(scales.shape, F32),
            pltpu.VMEM((2, 2, ys, 2, 2, sub, units), BF16),
            pltpu.SemaphoreType.DMA((10,)),
        ],
        compiler_params=pltpu.CompilerParams(vmem_limit_bytes=58 * 2**20),
        cost_estimate=pl.CostEstimate(flops=flops, bytes_accessed=2 * size, transcendentals=0),
    )(start, tok, codes, scales)
    members = [
        [moved(n + 2 * q, l) for q in range(2) for l in range(locals_)]
        for n in range(nodes)
        if n & 2 == 0
    ]
    got = lax.all_to_all(
        partial.reshape(2 * locals_, 2 * mine, units),
        ("node", "local"), 0, 0, axis_index_groups=members, tiled=True,
    ).reshape(2, locals_, 2, mine, units)

    def piece(q, t):
        part = lax.dynamic_index_in_dim(
            lax.dynamic_index_in_dim(cot, q, 0, False), t, 1, False
        )
        return jnp.concatenate([weight, part.reshape(mine, units)], axis=0)

    p, z = par[0], side[0]
    far = send(piece(1 - p, z), piece(p, 1 - z), piece(1 - p, 1 - z))
    block = nodes // 4
    step = [
        (moved(n, l), moved(n + (block if l >= ys else nodes - block), (l + ys) % locals_))
        for n, l in spots
    ]
    leave = lax.dynamic_index_in_dim(lax.dynamic_index_in_dim(tok, p, 2, False), 1 - z, 3, False)
    far_tok = lax.ppermute(leave, ("node", "local"), step)
    got, far, far_tok = lax.optimization_barrier((got, far, far_tok))
    *acts, slope = call(
        functools.partial(activate, feat),
        [((mine, units), BF16)] * 4 + [((2, 2, mine, units), BF16)],
        [SMEM, SMEM] + [VMEM] * 5,
        rows * units * 4, size,
        par, side, got, cot, *far,
    )
    lines = [list(range(t * ys, (t + 1) * ys)) for t in range(2)]
    spread = lax.all_gather(
        slope.reshape(4 * mine, units), "local", axis=0, tiled=True, axis_index_groups=lines
    ).reshape(ys, 2, 2, 2, sub, units)
    weights = (weight,) + tuple(far)
    (other,) = call(
        back_other,
        [((2, rows // 8, feat), BF16)],
        [SMEM] + [VMEM] * 5,
        flops // 2, size,
        core, spread, *weights,
    )
    other = lax.ppermute(other, "node", [(i, i ^ 1) for i in range(nodes)])
    shares = call(
        weigh_far,
        [((feat, units), BF16)] * 3,
        [SMEM, SMEM, VMEM, VMEM, VMEM],
        flops // 2, size,
        par, side, tok, far_tok, spread,
    )
    shares = send(*shares)
    (both,) = call(
        back_mine,
        [((2, 2, 2, ys // 2, sub, feat), BF16)],
        [SMEM, SMEM] + [VMEM] * 6,
        flops // 2, size,
        core, side, spread, *weights, other,
    )
    both, acts = lax.optimization_barrier((both, acts))
    groups = [
        [
            moved(per * (ys * t + y) + low, k * ys + own)
            for t in range(2)
            for m in range(2)
            for k in range(2)
            for y in range(m * ys // 2, (m + 1) * ys // 2)
        ]
        for low in range(per)
        for own in range(ys)
    ]
    sums = lax.all_to_all(
        both.reshape(nodes // 2, sub, feat),
        ("node", "local"), 0, 0, axis_index_groups=groups, tiled=True,
    ).reshape(4, 2, nodes // 16, sub, feat)
    (weight_grad,) = call(
        functools.partial(weigh_own, rows ** (-0.5)),
        [((feat, units), F32)],
        [SMEM, SMEM] + [VMEM] * 5,
        10 * flops, size,
        par, side, tok, spread, *shares,
    )
    (input_grad,) = call(
        finish, [((2, sub, feat), BF16)], [VMEM], rows * feat, size // 2, sums
    )
    (act,) = call(
        gather,
        [((2, 2, 2, sub, units), BF16)],
        [SMEM, SMEM] + [VMEM] * 4,
        rows * units // locals_, size // locals_,
        par, side, acts[0], *send(*acts[1:]),
    )
    return (
        act.reshape(rows // locals_, units),
        input_grad.reshape(rows // nodes, feat),
        weight_grad,
    )


def solution(mesh):
    body = functools.partial(shards, mesh.shape["local"], mesh.shape["node"])
    placed = (P(None, "local"), P("local", "node"), P(None, "node"), P("local", "node"))
    return jax.shard_map(
        lambda *args: body(*args),
        mesh=mesh,
        in_specs=placed,
        out_specs=(P("local", "node"), P("node", "local"), P("local", "node")),
        check_vma=False,
    )
```

```python
import functools
import math

import jax
import jax.numpy as jnp
from jax import lax
from jax.experimental import pallas as pl
from jax.experimental.pallas import tpu as pltpu
from jax.sharding import PartitionSpec as P

BLOCK = 2048
F32 = jnp.float32
BF16 = jnp.bfloat16
ROOT = math.sqrt(2.0 / math.pi)
VMEM = pl.BlockSpec(memory_space=pltpu.VMEM)
SMEM = pl.BlockSpec(memory_space=pltpu.SMEM)


def call(kernel, outs, specs, flops, size, *args):
    return pl.pallas_call(
        kernel,
        out_shape=[jax.ShapeDtypeStruct(s, d) for s, d in outs],
        in_specs=specs,
        out_specs=[VMEM] * len(outs),
        compiler_params=pltpu.CompilerParams(vmem_limit_bytes=40 * 2**20),
        cost_estimate=pl.CostEstimate(flops=flops, bytes_accessed=size, transcendentals=0),
    )(*args)


HBM = pl.BlockSpec(memory_space=pltpu.HBM)


def project(start_ref, tok_hbm, codes_hbm, scales_hbm, w_ref, out_hbm, tok_ref, codes_ref, scales_ref, out_ref, sems):
    feat, units = codes_ref.shape
    cuts = [(z, y) for z in range(2) for y in (0, 1)]
    span = tok_ref.shape[1] // 2
    first = [
        pltpu.make_async_copy(codes_hbm, codes_ref, sems.at[0]),
        pltpu.make_async_copy(scales_hbm, scales_ref, sems.at[1]),
    ]
    loads = [
        pltpu.make_async_copy(
            tok_hbm.at[z, pl.ds(y * span, span)],
            tok_ref.at[z, pl.ds(y * span, span)],
            sems.at[2 + i],
        )
        for i, (z, y) in enumerate(cuts)
    ]
    for copy in first + loads:
        copy.start()
    for copy in first:
        copy.wait()
    row = start_ref[0] + lax.broadcasted_iota(jnp.int32, (feat, units), 0)
    scale = jnp.broadcast_to(scales_ref[0:1, :], (feat, units))
    for i in range(1, scales_ref.shape[0]):
        scale = jnp.where(row >= i * BLOCK, scales_ref[i : i + 1, :], scale)
    weight = (codes_ref[...].astype(F32) * scale).astype(BF16)
    w_ref[...] = weight
    stores = []
    for i, ((z, y), copy) in enumerate(zip(cuts, loads)):
        copy.wait()
        ys = slice(y * span, (y + 1) * span)
        piece = tok_ref[z, ys]
        res = jnp.dot(piece.reshape(-1, feat), weight, preferred_element_type=F32)
        res = res.astype(BF16).reshape(piece.shape[:-1] + (units,))
        for q in range(2):
            for h in range(2):
                out_ref[q, h, ys, z] = res[:, q, :, h]
        part = pl.ds(y * span, span)
        store = pltpu.make_async_copy(
            out_ref.at[:, :, part, z], out_hbm.at[:, :, part, z], sems.at[6 + i]
        )
        store.start()
        stores.append(store)
    for store in stores:
        store.wait()


def activate(feat, par_ref, side_ref, got_ref, *refs):
    cots, acts, slope_ref = refs[:4], refs[4:8], refs[8]
    par, side = par_ref[0], side_ref[0]
    for i in range(4):
        unit, half = i % 2, i // 2
        q = par if unit == 0 else 1 - par
        t = side if half == 0 else 1 - side
        pre = jnp.sum(got_ref[q, :, t].astype(F32), axis=0)
        cot = cots[i][par, :, side] if i == 0 else cots[i][feat:, :]
        cot = cot.reshape(pre.shape).astype(F32)
        square = pre * pre
        tanh = jnp.tanh(ROOT * (pre + 0.044715 * square * pre))
        acts[i][...] = (0.5 * pre * (1.0 + tanh)).astype(BF16)
        inner = ROOT * (1.0 + 3.0 * 0.044715 * square)
        grad = 0.5 * (1.0 + tanh) + 0.5 * pre * (1.0 - tanh * tanh) * inner
        slope = (cot * grad).astype(BF16)
        slope_ref[:, unit, t] = jnp.broadcast_to(slope[None], (slope_ref.shape[0],) + slope.shape)


def gather(par_ref, side_ref, own_ref, x_ref, z_ref, both_ref, out_ref):
    par, side = par_ref[0], side_ref[0]
    for i, ref in enumerate((own_ref, x_ref, z_ref, both_ref)):
        q = par if i % 2 == 0 else 1 - par
        t = side if i < 2 else 1 - side
        out_ref[q, :, t] = ref[...].reshape(out_ref.shape[1], *out_ref.shape[3:])


def back(core, slope_ref, weights, out_feat):
    total = None
    for unit, weight in enumerate(weights):
        rows = slope_ref[:, unit, :, core]
        part = lax.dot_general(
            rows.reshape(-1, rows.shape[-1]),
            weight[: out_feat, :],
            (((1,), (1,)), ((), ())),
            preferred_element_type=F32,
        )
        total = part if total is None else total + part
    return total


def back_other(core_ref, slope_ref, *refs):
    core, out_ref = 1 - core_ref[0], refs[4]
    for k in range(2):
        out_ref[k] = back(
            core, slope_ref, refs[2 * k : 2 * k + 2], out_ref.shape[-1]
        ).astype(BF16)


def back_mine(core_ref, side_ref, slope_ref, *refs):
    core, side = core_ref[0], side_ref[0]
    other_ref, out_ref = refs[4:]
    high, mid, _, wide, rows, feat = out_ref.shape
    for k in range(2):
        total = back(core, slope_ref, refs[2 * k : 2 * k + 2], feat)
        total = total + other_ref[k].astype(F32)
        which = side if k == 0 else 1 - side
        total = total.astype(BF16).reshape(mid, wide, high, rows, feat)
        for t in range(high):
            out_ref[t, :, which] = total[:, :, t]


def finish(got_ref, out_ref):
    for k in range(2):
        part = got_ref[:, k].astype(F32)
        out_ref[k] = jnp.sum(part.reshape((-1,) + part.shape[2:]), axis=0).astype(BF16)


def outer(toks, slope_ref, unit):
    total = None
    for z, rows in enumerate(toks):
        grads = slope_ref[:, unit, z]
        part = lax.dot_general(
            rows.reshape(-1, rows.shape[-1]),
            grads.reshape(-1, grads.shape[-1]),
            (((0,), (0,)), ((), ())),
            preferred_element_type=F32,
        )
        total = part if total is None else total + part
    return total


def weigh_far(par_ref, side_ref, tok_ref, far_tok_ref, slope_ref, x_ref, z_ref, both_ref):
    par, side = par_ref[0], side_ref[0]
    mine = [tok_ref[z, :, par, :, side] for z in range(2)]
    far = [far_tok_ref[z] for z in range(2)]
    z_ref[...] = outer(far, slope_ref, 0).astype(BF16)
    both_ref[...] = outer(far, slope_ref, 1).astype(BF16)
    x_ref[...] = outer(mine, slope_ref, 1).astype(BF16)


def weigh_own(factor, par_ref, side_ref, tok_ref, slope_ref, x_ref, z_ref, both_ref, out_ref):
    par, side = par_ref[0], side_ref[0]
    total = outer([tok_ref[z, :, par, :, side] for z in range(2)], slope_ref, 0)
    for ref in (x_ref, z_ref, both_ref):
        total = total + ref[...].astype(F32)
    out_ref[...] = total * factor


def shards(locals_, nodes, tokens, codes, scales, cotangent):
    rows, feat = tokens.shape
    units = codes.shape[1]
    ys = locals_ // 2
    per = nodes // locals_
    sub = rows // nodes // 2
    mine = 2 * sub
    node = lax.axis_index("node").astype(jnp.int32)
    local = lax.axis_index("local").astype(jnp.int32)
    start = (local * feat).reshape(1)
    core = (node % 2).reshape(1)
    par = (node // 2 % 2).reshape(1)
    side = (local // ys).reshape(1)
    tok = tokens.reshape(2, ys, 2, 2, 2, sub, feat)
    cot = cotangent.reshape(2, 2, 2, sub, units)
    flops = 2 * rows * feat * units
    size = 2 * rows * feat

    def moved(n, l):
        return n % nodes * locals_ + l

    spots = [(n, l) for n in range(nodes) for l in range(locals_)]
    over_x = [(i, i ^ 2) for i in range(nodes)]
    over_z = [(i, (i + ys) % locals_) for i in range(locals_)]
    over_both = [(moved(n, l), moved(n ^ 2, (l + ys) % locals_)) for n, l in spots]

    def send(x, z, both):
        return (
            lax.ppermute(x, "node", over_x),
            lax.ppermute(z, "local", over_z),
            lax.ppermute(both, ("node", "local"), over_both),
        )

    weight, partial = pl.pallas_call(
        project,
        out_shape=[
            jax.ShapeDtypeStruct((feat, units), BF16),
            jax.ShapeDtypeStruct((2, 2, ys, 2, 2, sub, units), BF16),
        ],
        in_specs=[SMEM, HBM, HBM, HBM],
        out_specs=[VMEM, HBM],
        scratch_shapes=[
            pltpu.VMEM(tok.shape, BF16),
            pltpu.VMEM(codes.shape, BF16),
            pltpu.VMEM(scales.shape, F32),
            pltpu.VMEM((2, 2, ys, 2, 2, sub, units), BF16),
            pltpu.SemaphoreType.DMA((10,)),
        ],
        compiler_params=pltpu.CompilerParams(vmem_limit_bytes=58 * 2**20),
        cost_estimate=pl.CostEstimate(flops=flops, bytes_accessed=2 * size, transcendentals=0),
    )(start, tok, codes, scales)
    members = [
        [moved(n + 2 * q, l) for q in range(2) for l in range(locals_)]
        for n in range(nodes)
        if n & 2 == 0
    ]
    got = lax.all_to_all(
        partial.reshape(2 * locals_, 2 * mine, units),
        ("node", "local"), 0, 0, axis_index_groups=members, tiled=True,
    ).reshape(2, locals_, 2, mine, units)

    def piece(q, t):
        part = lax.dynamic_index_in_dim(
            lax.dynamic_index_in_dim(cot, q, 0, False), t, 1, False
        )
        return jnp.concatenate([weight, part.reshape(mine, units)], axis=0)

    p, z = par[0], side[0]
    far = send(piece(1 - p, z), piece(p, 1 - z), piece(1 - p, 1 - z))
    block = nodes // 4
    step = [
        (moved(n, l), moved(n + (block if l >= ys else nodes - block), (l + ys) % locals_))
        for n, l in spots
    ]
    leave = lax.dynamic_index_in_dim(lax.dynamic_index_in_dim(tok, p, 2, False), 1 - z, 3, False)
    got, far = lax.optimization_barrier((got, far))
    *acts, slope = call(
        functools.partial(activate, feat),
        [((mine, units), BF16)] * 4 + [((ys, 2, 2, mine, units), BF16)],
        [SMEM, SMEM] + [VMEM] * 5,
        rows * units * 4, size,
        par, side, got, cot, *far,
    )
    lines = [list(range(t * ys, (t + 1) * ys)) for t in range(2)]
    spread = lax.all_to_all(
        slope.reshape(ys, 4 * mine, units), "local", 0, 0, axis_index_groups=lines, tiled=True
    ).reshape(ys, 2, 2, 2, sub, units)
    acts, leave = lax.optimization_barrier((acts, leave))
    far_tok = lax.ppermute(leave, ("node", "local"), step)
    (act,) = call(
        gather,
        [((2, 2, 2, sub, units), BF16)],
        [SMEM, SMEM] + [VMEM] * 4,
        rows * units // locals_, size // locals_,
        par, side, acts[0], *send(*acts[1:]),
    )
    spread, far_tok, act = lax.optimization_barrier((spread, far_tok, act))
    weights = (weight,) + tuple(far)
    (other,) = call(
        back_other,
        [((2, rows // 8, feat), BF16)],
        [SMEM] + [VMEM] * 5,
        flops // 2, size,
        core, spread, *weights,
    )
    other = lax.ppermute(other, "node", [(i, i ^ 1) for i in range(nodes)])
    shares = call(
        weigh_far,
        [((feat, units), BF16)] * 3,
        [SMEM, SMEM, VMEM, VMEM, VMEM],
        flops // 2, size,
        par, side, tok, far_tok, spread,
    )
    shares = send(*shares)
    (both,) = call(
        back_mine,
        [((2, 2, 2, ys // 2, sub, feat), BF16)],
        [SMEM, SMEM] + [VMEM] * 6,
        flops // 2, size,
        core, side, spread, *weights, other,
    )
    groups = [
        [
            moved(per * (ys * t + y) + low, k * ys + own)
            for t in range(2)
            for m in range(2)
            for k in range(2)
            for y in range(m * ys // 2, (m + 1) * ys // 2)
        ]
        for low in range(per)
        for own in range(ys)
    ]
    sums = lax.all_to_all(
        both.reshape(nodes // 2, sub, feat),
        ("node", "local"), 0, 0, axis_index_groups=groups, tiled=True,
    ).reshape(4, 2, nodes // 16, sub, feat)
    (weight_grad,) = call(
        functools.partial(weigh_own, rows ** (-0.5)),
        [((feat, units), F32)],
        [SMEM, SMEM] + [VMEM] * 5,
        10 * flops, size,
        par, side, tok, spread, *shares,
    )
    (input_grad,) = call(
        finish, [((2, sub, feat), BF16)], [VMEM], rows * feat, size // 2, sums
    )
    return (
        act.reshape(rows // locals_, units),
        input_grad.reshape(rows // nodes, feat),
        weight_grad,
    )


def solution(mesh):
    body = functools.partial(shards, mesh.shape["local"], mesh.shape["node"])
    placed = (P(None, "local"), P("local", "node"), P(None, "node"), P("local", "node"))
    return jax.shard_map(
        lambda *args: body(*args),
        mesh=mesh,
        in_specs=placed,
        out_specs=(P("local", "node"), P("node", "local"), P("local", "node")),
        check_vma=False,
    )
```

```python
import functools
import math

import jax
import jax.numpy as jnp
from jax import lax
from jax.experimental import pallas as pl
from jax.experimental.pallas import tpu as pltpu
from jax.sharding import PartitionSpec as P

BLOCK = 2048
F32 = jnp.float32
BF16 = jnp.bfloat16
ROOT = math.sqrt(2.0 / math.pi)
VMEM = pl.BlockSpec(memory_space=pltpu.VMEM)
SMEM = pl.BlockSpec(memory_space=pltpu.SMEM)


def call(kernel, outs, specs, flops, size, *args):
    return pl.pallas_call(
        kernel,
        out_shape=[jax.ShapeDtypeStruct(s, d) for s, d in outs],
        in_specs=specs,
        out_specs=[VMEM] * len(outs),
        compiler_params=pltpu.CompilerParams(vmem_limit_bytes=40 * 2**20),
        cost_estimate=pl.CostEstimate(flops=flops, bytes_accessed=size, transcendentals=0),
    )(*args)


HBM = pl.BlockSpec(memory_space=pltpu.HBM)


def project(start_ref, tok_hbm, codes_hbm, scales_hbm, w_ref, out_hbm, tok_ref, codes_ref, scales_ref, out_ref, sems):
    feat, units = codes_ref.shape
    cuts = [(z, y) for z in range(2) for y in (0, 1)]
    span = tok_ref.shape[1] // 2
    first = [
        pltpu.make_async_copy(codes_hbm, codes_ref, sems.at[0]),
        pltpu.make_async_copy(scales_hbm, scales_ref, sems.at[1]),
    ]
    loads = [
        pltpu.make_async_copy(
            tok_hbm.at[z, pl.ds(y * span, span)],
            tok_ref.at[z, pl.ds(y * span, span)],
            sems.at[2 + i],
        )
        for i, (z, y) in enumerate(cuts)
    ]
    for copy in first + loads:
        copy.start()
    for copy in first:
        copy.wait()
    row = start_ref[0] + lax.broadcasted_iota(jnp.int32, (feat, units), 0)
    scale = jnp.broadcast_to(scales_ref[0:1, :], (feat, units))
    for i in range(1, scales_ref.shape[0]):
        scale = jnp.where(row >= i * BLOCK, scales_ref[i : i + 1, :], scale)
    weight = (codes_ref[...].astype(F32) * scale).astype(BF16)
    w_ref[...] = weight
    stores = []
    for i, ((z, y), copy) in enumerate(zip(cuts, loads)):
        copy.wait()
        ys = slice(y * span, (y + 1) * span)
        piece = tok_ref[z, ys]
        res = jnp.dot(piece.reshape(-1, feat), weight, preferred_element_type=F32)
        res = res.astype(BF16).reshape(piece.shape[:-1] + (units,))
        for q in range(2):
            for h in range(2):
                out_ref[q, h, ys, z] = res[:, q, :, h]
        part = pl.ds(y * span, span)
        store = pltpu.make_async_copy(
            out_ref.at[:, :, part, z], out_hbm.at[:, :, part, z], sems.at[6 + i]
        )
        store.start()
        stores.append(store)
    for store in stores:
        store.wait()


def activate(feat, par_ref, side_ref, got_ref, *refs):
    cots, acts, slope_ref = refs[:4], refs[4:8], refs[8]
    par, side = par_ref[0], side_ref[0]
    for i in range(4):
        unit, half = i % 2, i // 2
        q = par if unit == 0 else 1 - par
        t = side if half == 0 else 1 - side
        pre = jnp.sum(got_ref[q, :, t].astype(F32), axis=0)
        cot = cots[i][par, :, side] if i == 0 else cots[i][feat:, :]
        cot = cot.reshape(pre.shape).astype(F32)
        square = pre * pre
        tanh = jnp.tanh(ROOT * (pre + 0.044715 * square * pre))
        acts[i][...] = (0.5 * pre * (1.0 + tanh)).astype(BF16)
        inner = ROOT * (1.0 + 3.0 * 0.044715 * square)
        grad = 0.5 * (1.0 + tanh) + 0.5 * pre * (1.0 - tanh * tanh) * inner
        slope = (cot * grad).astype(BF16)
        slope_ref[:, unit, t] = jnp.broadcast_to(slope[None], (slope_ref.shape[0],) + slope.shape)


def gather(par_ref, side_ref, own_ref, x_ref, z_ref, both_ref, out_ref):
    par, side = par_ref[0], side_ref[0]
    for i, ref in enumerate((own_ref, x_ref, z_ref, both_ref)):
        q = par if i % 2 == 0 else 1 - par
        t = side if i < 2 else 1 - side
        out_ref[q, :, t] = ref[...].reshape(out_ref.shape[1], *out_ref.shape[3:])


def back(core, slope_ref, weights, out_feat):
    total = None
    for unit, weight in enumerate(weights):
        rows = slope_ref[:, unit, :, core]
        part = lax.dot_general(
            rows.reshape(-1, rows.shape[-1]),
            weight[: out_feat, :],
            (((1,), (1,)), ((), ())),
            preferred_element_type=F32,
        )
        total = part if total is None else total + part
    return total


def back_other(core_ref, slope_ref, *refs):
    core, out_ref = 1 - core_ref[0], refs[4]
    for k in range(2):
        out_ref[k] = back(
            core, slope_ref, refs[2 * k : 2 * k + 2], out_ref.shape[-1]
        ).astype(BF16)


def back_mine(core_ref, side_ref, slope_ref, *refs):
    core, side = core_ref[0], side_ref[0]
    other_ref, out_ref = refs[4:]
    high, mid, _, wide, rows, feat = out_ref.shape
    for k in range(2):
        total = back(core, slope_ref, refs[2 * k : 2 * k + 2], feat)
        total = total + other_ref[k].astype(F32)
        which = side if k == 0 else 1 - side
        total = total.astype(BF16).reshape(mid, wide, high, rows, feat)
        for t in range(high):
            out_ref[t, :, which] = total[:, :, t]


def finish(got_ref, out_ref):
    for k in range(2):
        part = got_ref[:, k].astype(F32)
        out_ref[k] = jnp.sum(part.reshape((-1,) + part.shape[2:]), axis=0).astype(BF16)


def outer(toks, slope_ref, unit):
    total = None
    for z, rows in enumerate(toks):
        grads = slope_ref[:, unit, z]
        part = lax.dot_general(
            rows.reshape(-1, rows.shape[-1]),
            grads.reshape(-1, grads.shape[-1]),
            (((0,), (0,)), ((), ())),
            preferred_element_type=F32,
        )
        total = part if total is None else total + part
    return total


def weigh_far(par_ref, side_ref, tok_ref, far_tok_ref, slope_ref, x_ref, z_ref, both_ref):
    par, side = par_ref[0], side_ref[0]
    mine = [tok_ref[z, :, par, :, side] for z in range(2)]
    far = [far_tok_ref[z] for z in range(2)]
    z_ref[...] = outer(far, slope_ref, 0).astype(BF16)
    both_ref[...] = outer(far, slope_ref, 1).astype(BF16)
    x_ref[...] = outer(mine, slope_ref, 1).astype(BF16)


def weigh_own(par_ref, side_ref, tok_ref, slope_ref, out_ref):
    par, side = par_ref[0], side_ref[0]
    out_ref[...] = outer([tok_ref[z, :, par, :, side] for z in range(2)], slope_ref, 0)


def join(factor, own_ref, x_ref, z_ref, both_ref, out_ref):
    total = own_ref[...]
    for ref in (x_ref, z_ref, both_ref):
        total = total + ref[...].astype(F32)
    out_ref[...] = total * factor


def shards(locals_, nodes, tokens, codes, scales, cotangent):
    rows, feat = tokens.shape
    units = codes.shape[1]
    ys = locals_ // 2
    per = nodes // locals_
    sub = rows // nodes // 2
    mine = 2 * sub
    node = lax.axis_index("node").astype(jnp.int32)
    local = lax.axis_index("local").astype(jnp.int32)
    start = (local * feat).reshape(1)
    core = (node % 2).reshape(1)
    par = (node // 2 % 2).reshape(1)
    side = (local // ys).reshape(1)
    tok = tokens.reshape(2, ys, 2, 2, 2, sub, feat)
    cot = cotangent.reshape(2, 2, 2, sub, units)
    flops = 2 * rows * feat * units
    size = 2 * rows * feat

    def moved(n, l):
        return n % nodes * locals_ + l

    spots = [(n, l) for n in range(nodes) for l in range(locals_)]
    over_x = [(i, i ^ 2) for i in range(nodes)]
    over_z = [(i, (i + ys) % locals_) for i in range(locals_)]
    over_both = [(moved(n, l), moved(n ^ 2, (l + ys) % locals_)) for n, l in spots]

    def send(x, z, both):
        return (
            lax.ppermute(x, "node", over_x),
            lax.ppermute(z, "local", over_z),
            lax.ppermute(both, ("node", "local"), over_both),
        )

    weight, partial = pl.pallas_call(
        project,
        out_shape=[
            jax.ShapeDtypeStruct((feat, units), BF16),
            jax.ShapeDtypeStruct((2, 2, ys, 2, 2, sub, units), BF16),
        ],
        in_specs=[SMEM, HBM, HBM, HBM],
        out_specs=[VMEM, HBM],
        scratch_shapes=[
            pltpu.VMEM(tok.shape, BF16),
            pltpu.VMEM(codes.shape, BF16),
            pltpu.VMEM(scales.shape, F32),
            pltpu.VMEM((2, 2, ys, 2, 2, sub, units), BF16),
            pltpu.SemaphoreType.DMA((10,)),
        ],
        compiler_params=pltpu.CompilerParams(vmem_limit_bytes=58 * 2**20),
        cost_estimate=pl.CostEstimate(flops=flops, bytes_accessed=2 * size, transcendentals=0),
    )(start, tok, codes, scales)
    members = [
        [moved(n + 2 * q, l) for q in range(2) for l in range(locals_)]
        for n in range(nodes)
        if n & 2 == 0
    ]
    got = lax.all_to_all(
        partial.reshape(2 * locals_, 2 * mine, units),
        ("node", "local"), 0, 0, axis_index_groups=members, tiled=True,
    ).reshape(2, locals_, 2, mine, units)

    def piece(q, t):
        part = lax.dynamic_index_in_dim(
            lax.dynamic_index_in_dim(cot, q, 0, False), t, 1, False
        )
        return jnp.concatenate([weight, part.reshape(mine, units)], axis=0)

    p, z = par[0], side[0]
    far = send(piece(1 - p, z), piece(p, 1 - z), piece(1 - p, 1 - z))
    block = nodes // 4
    step = [
        (moved(n, l), moved(n + (block if l >= ys else nodes - block), (l + ys) % locals_))
        for n, l in spots
    ]
    leave = lax.dynamic_index_in_dim(lax.dynamic_index_in_dim(tok, p, 2, False), 1 - z, 3, False)
    got, far = lax.optimization_barrier((got, far))
    *acts, slope = call(
        functools.partial(activate, feat),
        [((mine, units), BF16)] * 4 + [((ys, 2, 2, mine, units), BF16)],
        [SMEM, SMEM] + [VMEM] * 5,
        rows * units * 4, size,
        par, side, got, cot, *far,
    )
    lines = [list(range(t * ys, (t + 1) * ys)) for t in range(2)]
    spread = lax.all_to_all(
        slope.reshape(ys, 4 * mine, units), "local", 0, 0, axis_index_groups=lines, tiled=True
    ).reshape(ys, 2, 2, 2, sub, units)
    acts, leave = lax.optimization_barrier((acts, leave))
    far_tok = lax.ppermute(leave, ("node", "local"), step)
    (act,) = call(
        gather,
        [((2, 2, 2, sub, units), BF16)],
        [SMEM, SMEM] + [VMEM] * 4,
        rows * units // locals_, size // locals_,
        par, side, acts[0], *send(*acts[1:]),
    )
    spread, far_tok, act = lax.optimization_barrier((spread, far_tok, act))
    weights = (weight,) + tuple(far)
    (other,) = call(
        back_other,
        [((2, rows // 8, feat), BF16)],
        [SMEM] + [VMEM] * 5,
        flops // 2, size,
        core, spread, *weights,
    )
    other = lax.ppermute(other, "node", [(i, i ^ 1) for i in range(nodes)])
    shares = call(
        weigh_far,
        [((feat, units), BF16)] * 3,
        [SMEM, SMEM, VMEM, VMEM, VMEM],
        flops // 2, size,
        par, side, tok, far_tok, spread,
    )
    share_x, share_z, share_both = shares
    share_z = lax.ppermute(share_z, "local", over_z)
    (both,) = call(
        back_mine,
        [((2, 2, 2, ys // 2, sub, feat), BF16)],
        [SMEM, SMEM] + [VMEM] * 6,
        flops // 2, size,
        core, side, spread, *weights, other,
    )
    share_z, share_x, share_both = lax.optimization_barrier((share_z, share_x, share_both))
    share_x = lax.ppermute(share_x, "node", over_x)
    share_both = lax.ppermute(share_both, ("node", "local"), over_both)
    groups = [
        [
            moved(per * (ys * t + y) + low, k * ys + own)
            for t in range(2)
            for m in range(2)
            for k in range(2)
            for y in range(m * ys // 2, (m + 1) * ys // 2)
        ]
        for low in range(per)
        for own in range(ys)
    ]
    sums = lax.all_to_all(
        both.reshape(nodes // 2, sub, feat),
        ("node", "local"), 0, 0, axis_index_groups=groups, tiled=True,
    ).reshape(4, 2, nodes // 16, sub, feat)
    (own,) = call(
        weigh_own,
        [((feat, units), F32)],
        [SMEM, SMEM, VMEM, VMEM],
        flops // 2, size,
        par, side, tok, spread,
    )
    (weight_grad,) = call(
        functools.partial(join, rows ** (-0.5)),
        [((feat, units), F32)],
        [VMEM] * 4,
        8 * flops, size,
        own, share_x, share_z, share_both,
    )
    (input_grad,) = call(
        finish, [((2, sub, feat), BF16)], [VMEM], rows * feat, size // 2, sums
    )
    return (
        act.reshape(rows // locals_, units),
        input_grad.reshape(rows // nodes, feat),
        weight_grad,
    )


def solution(mesh):
    body = functools.partial(shards, mesh.shape["local"], mesh.shape["node"])
    placed = (P(None, "local"), P("local", "node"), P(None, "node"), P("local", "node"))
    return jax.shard_map(
        lambda *args: body(*args),
        mesh=mesh,
        in_specs=placed,
        out_specs=(P("local", "node"), P("node", "local"), P("local", "node")),
        check_vma=False,
    )
```

```python
import functools
import math

import jax
import jax.numpy as jnp
from jax import lax
from jax.experimental import pallas as pl
from jax.experimental.pallas import tpu as pltpu
from jax.sharding import PartitionSpec as P

BLOCK = 2048
F32 = jnp.float32
BF16 = jnp.bfloat16
ROOT = math.sqrt(2.0 / math.pi)
VMEM = pl.BlockSpec(memory_space=pltpu.VMEM)
SMEM = pl.BlockSpec(memory_space=pltpu.SMEM)


def call(kernel, outs, specs, flops, size, *args):
    return pl.pallas_call(
        kernel,
        out_shape=[jax.ShapeDtypeStruct(s, d) for s, d in outs],
        in_specs=specs,
        out_specs=[VMEM] * len(outs),
        compiler_params=pltpu.CompilerParams(vmem_limit_bytes=40 * 2**20),
        cost_estimate=pl.CostEstimate(flops=flops, bytes_accessed=size, transcendentals=0),
    )(*args)


HBM = pl.BlockSpec(memory_space=pltpu.HBM)


def project(start_ref, tok_hbm, codes_hbm, scales_hbm, w_hbm, out_hbm, tok_ref, codes_ref, scales_ref, w_ref, out_ref, sems):
    feat, units = codes_ref.shape
    cuts = [(z, y) for z in range(2) for y in (0, 1)]
    span = tok_ref.shape[1] // 2
    first = [
        pltpu.make_async_copy(codes_hbm, codes_ref, sems.at[0]),
        pltpu.make_async_copy(scales_hbm, scales_ref, sems.at[1]),
    ]
    loads = [
        pltpu.make_async_copy(
            tok_hbm.at[z, pl.ds(y * span, span)],
            tok_ref.at[z, pl.ds(y * span, span)],
            sems.at[2 + i],
        )
        for i, (z, y) in enumerate(cuts)
    ]
    for copy in first + loads:
        copy.start()
    for copy in first:
        copy.wait()
    row = start_ref[0] + lax.broadcasted_iota(jnp.int32, (feat, units), 0)
    scale = jnp.broadcast_to(scales_ref[0:1, :], (feat, units))
    for i in range(1, scales_ref.shape[0]):
        scale = jnp.where(row >= i * BLOCK, scales_ref[i : i + 1, :], scale)
    weight = (codes_ref[...].astype(F32) * scale).astype(BF16)
    w_ref[...] = weight
    stores = [pltpu.make_async_copy(w_ref, w_hbm, sems.at[10])]
    stores[0].start()
    for i, ((z, y), copy) in enumerate(zip(cuts, loads)):
        copy.wait()
        ys = slice(y * span, (y + 1) * span)
        piece = tok_ref[z, ys]
        res = jnp.dot(piece.reshape(-1, feat), weight, preferred_element_type=F32)
        res = res.astype(BF16).reshape(piece.shape[:-1] + (units,))
        for h in range(2):
            out_ref[h, ys, z] = res[:, :, h]
        part = pl.ds(y * span, span)
        store = pltpu.make_async_copy(
            out_ref.at[:, part, z], out_hbm.at[:, part, z], sems.at[6 + i]
        )
        store.start()
        stores.append(store)
    for store in stores:
        store.wait()


def activate(side_ref, got_ref, cot_ref, far_cot_ref, act_ref, far_act_ref, slope_ref):
    side = side_ref[0]
    for k in range(2):
        which = side if k == 0 else 1 - side
        pre = jnp.sum(got_ref[:, which].astype(F32), axis=0)
        cot = cot_ref[:, side] if k == 0 else far_cot_ref[...]
        cot = cot.reshape(pre.shape).astype(F32)
        square = pre * pre
        tanh = jnp.tanh(ROOT * (pre + 0.044715 * square * pre))
        act = (0.5 * pre * (1.0 + tanh)).astype(BF16)
        if k == 0:
            act_ref[...] = act
        else:
            far_act_ref[...] = act
        inner = ROOT * (1.0 + 3.0 * 0.044715 * square)
        grad = 0.5 * (1.0 + tanh) + 0.5 * pre * (1.0 - tanh * tanh) * inner
        slope_ref[which] = (cot * grad).astype(BF16)


def back(core, slope_ref, w_ref):
    rows = slope_ref[:, :, :, core]
    return lax.dot_general(
        rows.reshape(-1, rows.shape[-1]),
        w_ref[...],
        (((1,), (1,)), ((), ())),
        preferred_element_type=F32,
    )


def back_other(core_ref, slope_ref, w_ref, far_w_ref, out_ref):
    core = 1 - core_ref[0]
    for k, weight in enumerate((w_ref, far_w_ref)):
        out_ref[k] = back(core, slope_ref, weight).astype(BF16)


def back_mine(core_ref, side_ref, slope_ref, w_ref, far_w_ref, other_ref, out_ref):
    core, side = core_ref[0], side_ref[0]
    for k, weight in enumerate((w_ref, far_w_ref)):
        total = back(core, slope_ref, weight) + other_ref[k].astype(F32)
        which = side if k == 0 else 1 - side
        high, mid, _, wide, low, rows, feat = out_ref.shape
        total = total.astype(BF16).reshape(mid, wide, high, low, rows, feat)
        for t in range(high):
            out_ref[t, :, which] = total[:, :, t]


def finish(got_ref, out_ref):
    for k in range(2):
        part = got_ref[:, k].astype(F32)
        out_ref[k] = jnp.sum(part.reshape((-1,) + part.shape[2:]), axis=0).astype(BF16)


def outer(rows, grads):
    return lax.dot_general(
        rows.reshape(-1, rows.shape[-1]),
        grads.reshape(-1, grads.shape[-1]),
        (((0,), (0,)), ((), ())),
        preferred_element_type=F32,
    )


def weigh_far(far_tok_ref, slope_ref, out_ref):
    total = sum(outer(far_tok_ref[z], slope_ref[:, z]) for z in range(2))
    out_ref[...] = total.astype(BF16)


def weigh_own(factor, side_ref, tok_ref, slope_ref, far_ref, out_ref):
    side = side_ref[0]
    total = sum(outer(tok_ref[z, :, :, side], slope_ref[:, z]) for z in range(2))
    out_ref[...] = (total + far_ref[...].astype(F32)) * factor


def shards(locals_, nodes, tokens, codes, scales, cotangent):
    rows, feat = tokens.shape
    units = codes.shape[1]
    ys = locals_ // 2
    per = nodes // locals_
    sub = rows // nodes // 2
    mine = per * sub
    node = lax.axis_index("node").astype(jnp.int32)
    local = lax.axis_index("local").astype(jnp.int32)
    start = (local * feat).reshape(1)
    core = (node % 2).reshape(1)
    side = (local // ys).reshape(1)
    tok = tokens.reshape(2, ys, per, 2, sub, feat)
    cot = cotangent.reshape(per, 2, sub, units)
    pair = [(i, (i + ys) % locals_) for i in range(locals_)]
    flops = 2 * rows * feat * units
    size = 2 * rows * feat

    weight, partial = pl.pallas_call(
        project,
        out_shape=[
            jax.ShapeDtypeStruct((feat, units), BF16),
            jax.ShapeDtypeStruct((2, ys, 2, per, sub, units), BF16),
        ],
        in_specs=[SMEM, HBM, HBM, HBM],
        out_specs=[HBM, HBM],
        scratch_shapes=[
            pltpu.VMEM(tok.shape, BF16),
            pltpu.VMEM(codes.shape, BF16),
            pltpu.VMEM(scales.shape, F32),
            pltpu.VMEM(codes.shape, BF16),
            pltpu.VMEM((2, ys, 2, per, sub, units), BF16),
            pltpu.SemaphoreType.DMA((11,)),
        ],
        compiler_params=pltpu.CompilerParams(vmem_limit_bytes=58 * 2**20),
        cost_estimate=pl.CostEstimate(flops=flops, bytes_accessed=2 * size, transcendentals=0),
    )(start, tok, codes, scales)
    got = lax.all_to_all(
        partial.reshape(locals_, 2 * mine, units), "local", 0, 0, tiled=True
    ).reshape(locals_, 2, mine, units)
    far_cot = lax.ppermute(
        lax.dynamic_index_in_dim(cot, 1 - side[0], 1, False), "local", pair
    )
    far_weight = lax.ppermute(weight, "local", pair)
    block = nodes // 4
    step = [
        (n * locals_ + l, (n + (block if l >= ys else -block)) % nodes * locals_ + (l + ys) % locals_)
        for n in range(nodes)
        for l in range(locals_)
    ]
    far_tok = lax.ppermute(
        lax.dynamic_index_in_dim(tok, 1 - side[0], 3, False), ("node", "local"), step
    )
    got, far_cot, far_weight, far_tok = lax.optimization_barrier(
        (got, far_cot, far_weight, far_tok)
    )
    act_own, act_far, slope = call(
        activate,
        [((mine, units), BF16), ((mine, units), BF16), ((2, mine, units), BF16)],
        [SMEM, VMEM, VMEM, VMEM],
        rows * units * 4, size,
        side, got, cot, far_cot,
    )
    lines = [list(range(z * ys, (z + 1) * ys)) for z in range(2)]
    spread = lax.all_gather(
        slope.reshape(2 * mine, units), "local", axis=0, tiled=True, axis_index_groups=lines
    )
    by_core = spread.reshape(ys, 2, per // 2, 2, sub, units)
    by_side = spread.reshape(ys, 2, per, sub, units)
    (other,) = call(
        back_other,
        [((2, rows // 4, feat), BF16)],
        [SMEM, VMEM, VMEM, VMEM],
        flops // 2, size,
        core, by_core, weight, far_weight,
    )
    other = lax.ppermute(other, "node", [(i, i ^ 1) for i in range(nodes)])
    (far_part,) = call(
        weigh_far, [((feat, units), BF16)], [VMEM, VMEM], flops // 2, size, far_tok, by_side
    )
    far_part = lax.ppermute(far_part, "local", pair)
    (both,) = call(
        back_mine,
        [((2, 2, 2, ys // 2, per // 2, sub, feat), BF16)],
        [SMEM, SMEM, VMEM, VMEM, VMEM, VMEM],
        flops // 2, size,
        core, side, by_core, weight, far_weight, other,
    )
    both, act_far = lax.optimization_barrier((both, act_far))
    groups = [
        [
            (per * (ys * t + y) + 2 * h + c) * locals_ + z * ys + own
            for t in range(2)
            for m in range(2)
            for z in range(2)
            for y in range(m * ys // 2, (m + 1) * ys // 2)
            for h in range(per // 2)
        ]
        for c in range(2)
        for own in range(ys)
    ]
    sums = lax.all_to_all(
        both.reshape(nodes, sub, feat),
        ("node", "local"), 0, 0, axis_index_groups=groups, tiled=True,
    ).reshape(4, 2, nodes // 8, sub, feat)
    (weight_grad,) = call(
        functools.partial(weigh_own, rows ** (-0.5)),
        [((feat, units), F32)],
        [SMEM, VMEM, VMEM, VMEM],
        20 * flops, size,
        side, tok, by_side, far_part,
    )
    (input_grad,) = call(
        finish, [((2, sub, feat), BF16)], [VMEM], rows * feat, size // 2, sums
    )
    act_far = lax.ppermute(act_far, "local", pair)
    first = side[0] == 0
    act_own, act_far = act_own.reshape(per, sub, units), act_far.reshape(per, sub, units)
    act = jnp.stack(
        [jnp.where(first, act_own, act_far), jnp.where(first, act_far, act_own)], axis=1
    )
    return (
        act.reshape(rows // locals_, units),
        input_grad.reshape(rows // nodes, feat),
        weight_grad,
    )


def solution(mesh):
    body = functools.partial(shards, mesh.shape["local"], mesh.shape["node"])
    placed = (P(None, "local"), P("local", "node"), P(None, "node"), P("local", "node"))
    return jax.shard_map(
        lambda *args: body(*args),
        mesh=mesh,
        in_specs=placed,
        out_specs=(P("local", "node"), P("node", "local"), P("local", "node")),
        check_vma=False,
    )
```

```python
import functools
import math

import jax
import jax.numpy as jnp
from jax import lax
from jax.experimental import pallas as pl
from jax.experimental.pallas import tpu as pltpu
from jax.sharding import PartitionSpec as P

BLOCK = 2048
F32 = jnp.float32
BF16 = jnp.bfloat16
ROOT = math.sqrt(2.0 / math.pi)
VMEM = pl.BlockSpec(memory_space=pltpu.VMEM)
SMEM = pl.BlockSpec(memory_space=pltpu.SMEM)


def call(kernel, outs, specs, flops, size, *args):
    return pl.pallas_call(
        kernel,
        out_shape=[jax.ShapeDtypeStruct(s, d) for s, d in outs],
        in_specs=specs,
        out_specs=[VMEM] * len(outs),
        compiler_params=pltpu.CompilerParams(vmem_limit_bytes=40 * 2**20),
        cost_estimate=pl.CostEstimate(flops=flops, bytes_accessed=size, transcendentals=0),
    )(*args)


HBM = pl.BlockSpec(memory_space=pltpu.HBM)


def project(start_ref, tok_hbm, codes_hbm, scales_hbm, w_hbm, out_hbm, tok_ref, codes_ref, scales_ref, w_ref, out_ref, sems):
    feat, units = codes_ref.shape
    cuts = [(z, y) for z in range(2) for y in range(4)]
    span = tok_ref.shape[1] // 4
    first = [
        pltpu.make_async_copy(codes_hbm, codes_ref, sems.at[0]),
        pltpu.make_async_copy(scales_hbm, scales_ref, sems.at[1]),
    ]
    loads = [
        pltpu.make_async_copy(
            tok_hbm.at[z, pl.ds(y * span, span)],
            tok_ref.at[z, pl.ds(y * span, span)],
            sems.at[2 + i],
        )
        for i, (z, y) in enumerate(cuts)
    ]
    for copy in first + loads:
        copy.start()
    for copy in first:
        copy.wait()
    row = start_ref[0] + lax.broadcasted_iota(jnp.int32, (feat, units), 0)
    scale = jnp.broadcast_to(scales_ref[0:1, :], (feat, units))
    for i in range(1, scales_ref.shape[0]):
        scale = jnp.where(row >= i * BLOCK, scales_ref[i : i + 1, :], scale)
    weight = (codes_ref[...].astype(F32) * scale).astype(BF16)
    w_ref[...] = weight
    stores = [pltpu.make_async_copy(w_ref, w_hbm, sems.at[18])]
    stores[0].start()
    for i, ((z, y), copy) in enumerate(zip(cuts, loads)):
        copy.wait()
        ys = slice(y * span, (y + 1) * span)
        piece = tok_ref[z, ys]
        res = jnp.dot(piece.reshape(-1, feat), weight, preferred_element_type=F32)
        res = res.astype(BF16).reshape(piece.shape[:-1] + (units,))
        for h in range(2):
            out_ref[h, ys, z] = res[:, :, h]
        part = pl.ds(y * span, span)
        store = pltpu.make_async_copy(
            out_ref.at[:, part, z], out_hbm.at[:, part, z], sems.at[10 + i]
        )
        store.start()
        stores.append(store)
    for store in stores:
        store.wait()


def activate(side_ref, got_ref, cot_ref, far_cot_ref, act_ref, far_act_ref, slope_ref):
    side = side_ref[0]
    for k in range(2):
        which = side if k == 0 else 1 - side
        pre = jnp.sum(got_ref[:, which].astype(F32), axis=0)
        cot = cot_ref[:, side] if k == 0 else far_cot_ref[...]
        cot = cot.reshape(pre.shape).astype(F32)
        square = pre * pre
        tanh = jnp.tanh(ROOT * (pre + 0.044715 * square * pre))
        act = (0.5 * pre * (1.0 + tanh)).astype(BF16)
        if k == 0:
            act_ref[...] = act
        else:
            far_act_ref[...] = act
        inner = ROOT * (1.0 + 3.0 * 0.044715 * square)
        grad = 0.5 * (1.0 + tanh) + 0.5 * pre * (1.0 - tanh * tanh) * inner
        slope_ref[which] = (cot * grad).astype(BF16)


def back(core, slope_ref, w_ref):
    rows = slope_ref[:, :, :, core]
    return lax.dot_general(
        rows.reshape(-1, rows.shape[-1]),
        w_ref[...],
        (((1,), (1,)), ((), ())),
        preferred_element_type=F32,
    )


def back_other(core_ref, slope_ref, w_ref, far_w_ref, out_ref):
    core = 1 - core_ref[0]
    for k, weight in enumerate((w_ref, far_w_ref)):
        out_ref[k] = back(core, slope_ref, weight).astype(BF16)


def back_mine(core_ref, side_ref, slope_ref, w_ref, far_w_ref, other_ref, out_ref):
    core, side = core_ref[0], side_ref[0]
    for k, weight in enumerate((w_ref, far_w_ref)):
        total = back(core, slope_ref, weight) + other_ref[k].astype(F32)
        which = side if k == 0 else 1 - side
        high, mid, _, wide, low, rows, feat = out_ref.shape
        total = total.astype(BF16).reshape(mid, wide, high, low, rows, feat)
        for t in range(high):
            out_ref[t, :, which] = total[:, :, t]


def finish(got_ref, out_ref):
    for k in range(2):
        part = got_ref[:, k].astype(F32)
        out_ref[k] = jnp.sum(part.reshape((-1,) + part.shape[2:]), axis=0).astype(BF16)


def outer(rows, grads):
    return lax.dot_general(
        rows.reshape(-1, rows.shape[-1]),
        grads.reshape(-1, grads.shape[-1]),
        (((0,), (0,)), ((), ())),
        preferred_element_type=F32,
    )


def weigh_far(far_tok_ref, slope_ref, out_ref):
    total = sum(outer(far_tok_ref[z], slope_ref[:, z]) for z in range(2))
    out_ref[...] = total.astype(BF16)


def weigh_own(factor, side_ref, tok_ref, slope_ref, far_ref, out_ref):
    side = side_ref[0]
    total = sum(outer(tok_ref[z, :, :, side], slope_ref[:, z]) for z in range(2))
    out_ref[...] = (total + far_ref[...].astype(F32)) * factor


def shards(locals_, nodes, tokens, codes, scales, cotangent):
    rows, feat = tokens.shape
    units = codes.shape[1]
    ys = locals_ // 2
    per = nodes // locals_
    sub = rows // nodes // 2
    mine = per * sub
    node = lax.axis_index("node").astype(jnp.int32)
    local = lax.axis_index("local").astype(jnp.int32)
    start = (local * feat).reshape(1)
    core = (node % 2).reshape(1)
    side = (local // ys).reshape(1)
    tok = tokens.reshape(2, ys, per, 2, sub, feat)
    cot = cotangent.reshape(per, 2, sub, units)
    pair = [(i, (i + ys) % locals_) for i in range(locals_)]
    flops = 2 * rows * feat * units
    size = 2 * rows * feat

    weight, partial = pl.pallas_call(
        project,
        out_shape=[
            jax.ShapeDtypeStruct((feat, units), BF16),
            jax.ShapeDtypeStruct((2, ys, 2, per, sub, units), BF16),
        ],
        in_specs=[SMEM, HBM, HBM, HBM],
        out_specs=[HBM, HBM],
        scratch_shapes=[
            pltpu.VMEM(tok.shape, BF16),
            pltpu.VMEM(codes.shape, BF16),
            pltpu.VMEM(scales.shape, F32),
            pltpu.VMEM(codes.shape, BF16),
            pltpu.VMEM((2, ys, 2, per, sub, units), BF16),
            pltpu.SemaphoreType.DMA((19,)),
        ],
        compiler_params=pltpu.CompilerParams(vmem_limit_bytes=58 * 2**20),
        cost_estimate=pl.CostEstimate(flops=flops, bytes_accessed=2 * size, transcendentals=0),
    )(start, tok, codes, scales)
    got = lax.all_to_all(
        partial.reshape(locals_, 2 * mine, units), "local", 0, 0, tiled=True
    ).reshape(locals_, 2, mine, units)
    far_cot = lax.ppermute(
        lax.dynamic_index_in_dim(cot, 1 - side[0], 1, False), "local", pair
    )
    far_weight = lax.ppermute(weight, "local", pair)
    block = nodes // 4
    step = [
        (n * locals_ + l, (n + (block if l >= ys else -block)) % nodes * locals_ + (l + ys) % locals_)
        for n in range(nodes)
        for l in range(locals_)
    ]
    far_tok = lax.ppermute(
        lax.dynamic_index_in_dim(tok, 1 - side[0], 3, False), ("node", "local"), step
    )
    got, far_cot, far_weight, far_tok = lax.optimization_barrier(
        (got, far_cot, far_weight, far_tok)
    )
    act_own, act_far, slope = call(
        activate,
        [((mine, units), BF16), ((mine, units), BF16), ((2, mine, units), BF16)],
        [SMEM, VMEM, VMEM, VMEM],
        rows * units * 4, size,
        side, got, cot, far_cot,
    )
    lines = [list(range(z * ys, (z + 1) * ys)) for z in range(2)]
    spread = lax.all_gather(
        slope.reshape(2 * mine, units), "local", axis=0, tiled=True, axis_index_groups=lines
    )
    by_core = spread.reshape(ys, 2, per // 2, 2, sub, units)
    by_side = spread.reshape(ys, 2, per, sub, units)
    (other,) = call(
        back_other,
        [((2, rows // 4, feat), BF16)],
        [SMEM, VMEM, VMEM, VMEM],
        flops // 2, size,
        core, by_core, weight, far_weight,
    )
    other = lax.ppermute(other, "node", [(i, i ^ 1) for i in range(nodes)])
    (far_part,) = call(
        weigh_far, [((feat, units), BF16)], [VMEM, VMEM], flops // 2, size, far_tok, by_side
    )
    far_part = lax.ppermute(far_part, "local", pair)
    (both,) = call(
        back_mine,
        [((2, 2, 2, ys // 2, per // 2, sub, feat), BF16)],
        [SMEM, SMEM, VMEM, VMEM, VMEM, VMEM],
        flops // 2, size,
        core, side, by_core, weight, far_weight, other,
    )
    both, act_far = lax.optimization_barrier((both, act_far))
    groups = [
        [
            (per * (ys * t + y) + 2 * h + c) * locals_ + z * ys + own
            for t in range(2)
            for m in range(2)
            for z in range(2)
            for y in range(m * ys // 2, (m + 1) * ys // 2)
            for h in range(per // 2)
        ]
        for c in range(2)
        for own in range(ys)
    ]
    sums = lax.all_to_all(
        both.reshape(nodes, sub, feat),
        ("node", "local"), 0, 0, axis_index_groups=groups, tiled=True,
    ).reshape(4, 2, nodes // 8, sub, feat)
    (weight_grad,) = call(
        functools.partial(weigh_own, rows ** (-0.5)),
        [((feat, units), F32)],
        [SMEM, VMEM, VMEM, VMEM],
        20 * flops, size,
        side, tok, by_side, far_part,
    )
    (input_grad,) = call(
        finish, [((2, sub, feat), BF16)], [VMEM], rows * feat, size // 2, sums
    )
    act_far = lax.ppermute(act_far, "local", pair)
    first = side[0] == 0
    act_own, act_far = act_own.reshape(per, sub, units), act_far.reshape(per, sub, units)
    act = jnp.stack(
        [jnp.where(first, act_own, act_far), jnp.where(first, act_far, act_own)], axis=1
    )
    return (
        act.reshape(rows // locals_, units),
        input_grad.reshape(rows // nodes, feat),
        weight_grad,
    )


def solution(mesh):
    body = functools.partial(shards, mesh.shape["local"], mesh.shape["node"])
    placed = (P(None, "local"), P("local", "node"), P(None, "node"), P("local", "node"))
    return jax.shard_map(
        lambda *args: body(*args),
        mesh=mesh,
        in_specs=placed,
        out_specs=(P("local", "node"), P("node", "local"), P("local", "node")),
        check_vma=False,
    )
```
